128 devices in a mesh: cx: 8 (over z, core), cy: 16 (over y, x).
Axes of the slice: x: 4, y: 4, z: 4, core: 2. Of those that a mesh axis runs over, the one named last changes fastest.
Arguments:
- latent: float32 [128, 256, 256], P('cx', 'cy'), may hold values from -6 to 6
- observed: float32 [131072], P(('cx', 'cy')), may hold values from -12 to 12
- sigma: float32 [131072], P(('cx', 'cy')), may hold values from 0.5 to 1.5
- response: bfloat16 [65536, 64, 128], P(('cx', 'cy')), may hold values from -0.375 to 0.375
- offsets: int32 [64, 65536], P(None, ('cx', 'cy')), may hold values from 0 to 254
- fractions: float32 [64, 65536], P(None, ('cx', 'cy')), may hold values from 0 to 1
- tile_group: int32 [65536], P(('cx', 'cy')), may hold values from 0 to 7
- tile_slot: int32 [65536], P(('cx', 'cy')), may hold values from 0 to 511, as said below
- send_index: int32 [128, 128, 4], P(('cx', 'cy')), may hold values from -1 to 255, as said below
Outputs:
- gradient: float32 [128, 256, 256], P('cx', 'cy')
- predicted: float32 [131072], P(('cx', 'cy'))
The draws below stay inside these ranges and needn't reach their ends.
Inputs may be any that keep to these rules, and one draw needn't show every extreme that they name: `send_index`: entries are local column numbers of the sending device, or -1 for an empty slot; for each sender and receiver the used slots come first, 2 to 4 of them; every sender uses all 4 slots for some receiver, and some receiver gets all 4 slots from every sender. `tile_slot`: tile slot q names slot q % 4 from sender q // 4, a slot that this sender uses for this device.
All inputs are finite; a program needn't handle non-finite values.
Results may differ from the reference program's by a relative error of at most 0.0036.
Values may be sent and summed in bfloat16 or wider, within the bound.
A program may use at most 64 MiB of HBM per device.

```python
import math
import jax
import jax.numpy as jnp
from jax import lax

CXV = 16
CYV = 16
NZ = 256
STAR_TILE = 128
SAMPLES = 64
NDEV = 128
TILES_DEV = 512
CAP = 4
G_DEV = 8
NX = 128
NY = 256
TILES = 65536
STARS = 131072
N_CX = 8
N_CY = 16


def pair_counts(key):
    counts = jax.random.randint(jax.random.fold_in(key, 101), (NDEV, NDEV), (CAP + 1) // 2, CAP + 1)
    chosen = jax.random.randint(jax.random.fold_in(key, 202), (NDEV,), 0, NDEV)
    full_owner = jax.random.randint(jax.random.fold_in(key, 303), (), 0, NDEV)
    owners = jnp.arange(NDEV)[None, :]
    filled = (chosen[:, None] == owners) | (owners == full_owner)
    return jnp.where(filled, CAP, counts)


def used_slots(key):
    counts = pair_counts(key)
    return jnp.arange(CAP)[None, None, :] < counts[:, :, None]


def draw_send_index(key, part):
    used_mask = used_slots(key)
    flat_used = used_mask.reshape(NDEV, NDEV * CAP).astype(jnp.int32)
    used_rank = jnp.cumsum(flat_used, axis=1) - 1
    row_keys = jax.random.split(jax.random.fold_in(key, 404), NDEV)
    shuffled = jax.vmap(lambda row_key: jax.random.permutation(row_key, CXV * CYV))(row_keys)
    column_picks = jnp.take_along_axis(shuffled, jnp.maximum(used_rank, 0) % (CXV * CYV), axis=1)
    result = jnp.where(flat_used > 0, column_picks, -1)
    return result.reshape(NDEV, NDEV, CAP).astype(jnp.int32)


def draw_tile_slot(key, part):
    used_mask = used_slots(key)
    by_owner = used_mask.transpose(1, 0, 2).reshape(NDEV, NDEV * CAP)
    slot_ids = jnp.arange(NDEV * CAP).astype(jnp.int32)
    scores = jnp.where(by_owner, 0, NDEV * CAP).astype(jnp.int32) + slot_ids[None, :]
    slot_order = jnp.argsort(scores, axis=1, stable=True).astype(jnp.int32)
    used_count = jnp.sum(by_owner.astype(jnp.int32), axis=1)
    row_keys = jax.random.split(jax.random.fold_in(key, 505), NDEV)
    shuffled = jax.vmap(lambda row_key: jax.random.permutation(row_key, TILES_DEV))(row_keys)
    chosen_rank = shuffled % used_count[:, None]
    tile_slots = jnp.take_along_axis(slot_order, chosen_rank, axis=1)
    return tile_slots.reshape(-1).astype(jnp.int32)


def set_ends(array, own_key, low, high):
    longest = array.shape.index(max(array.shape))
    spots = []
    for shift in (0, 1):
        where = [jax.random.randint(jax.random.fold_in(own_key, axis), (), 0, length) for axis, length in enumerate(array.shape)]
        where[longest] = (where[longest] + shift) % array.shape[longest]
        spots.append(tuple(where))
    return array.at[spots[0]].set(low).at[spots[1]].set(high)


def shard_levels(own_key, dims, shards, smallest, high):
    loudness, own = 1.0, jax.random.fold_in(own_key, 6)
    for axis_at, parts in shards:
        steps = jnp.exp(jax.random.uniform(jax.random.fold_in(own, axis_at), (parts,), jnp.float32, smallest / len(shards), high / len(shards)))
        loudness = loudness * jnp.repeat(steps, dims[axis_at] // parts).reshape([-1 if axis == axis_at else 1 for axis in range(len(dims))])
    return loudness


def bell_draw(own_key, shape, spread, bound, shards=(), kind=jnp.bfloat16):
    values = spread * jax.random.normal(own_key, shape, jnp.float32)
    if shards:
        values = values * shard_levels(own_key, shape, shards, -0.22, 0.18)
    return jnp.clip(values, -bound, bound).astype(kind)


def setup_inputs(seed: int = 0) -> dict:
    key_of = jax.random.split(jax.random.key(seed), 10)
    latent = bell_draw(key_of[0], (NX, NY, NZ), 1.0, 6.0, ((0, 8), (1, 16)), jnp.float32)
    observed = bell_draw(key_of[1], (STARS,), 2.0, 12.0, ((0, 128),), jnp.float32)
    sigma = jnp.clip(jnp.exp(math.log(1.5) - 1.0986123 * jax.random.uniform(key_of[2], (STARS,), jnp.float32) ** shard_levels(key_of[2], (STARS,), ((0, 128),), -0.2, 0.2)), 0.5, 1.5)
    response = bell_draw(key_of[3], (TILES, SAMPLES, STAR_TILE), (4 * SAMPLES) ** -0.5, 0.375, ((0, 128),))
    offsets = set_ends(jax.random.randint(key_of[4], (SAMPLES, TILES), 0, NZ - 1), jax.random.fold_in(key_of[4], 1), 0, (NZ - 1) - 1).astype(jnp.int32)
    fractions = jnp.clip(1.0 * jax.random.uniform(key_of[5], (SAMPLES, TILES), jnp.float32) ** shard_levels(key_of[5], (SAMPLES, TILES), ((1, 128),), -0.2, 0.2), 0.0, 1.0)
    tile_group = set_ends(jax.random.randint(key_of[6], (TILES,), 0, G_DEV), jax.random.fold_in(key_of[6], 1), 0, G_DEV - 1).astype(jnp.int32)
    tile_slot = draw_tile_slot(jax.random.fold_in(key_of[9], 71), 0)
    send_index = draw_send_index(jax.random.fold_in(key_of[9], 71), 0)
    return {"latent": latent, "observed": observed, "sigma": sigma, "response": response, "offsets": offsets, "fractions": fractions, "tile_group": tile_group, "tile_slot": tile_slot, "send_index": send_index}


def kernel_taps():
    shifts = jnp.arange(-16, 17).astype(jnp.float32)
    scaled = jnp.sqrt(jnp.float32(3.0)) * jnp.abs(shifts) / 8.0
    raw_taps = (1.0 + scaled) * jnp.exp(-scaled)
    return 0.8 * raw_taps / jnp.sqrt(jnp.sum(raw_taps * raw_taps))

def taps_along(values, along, kernel):
    length = values.shape[along]
    padding = [(0, 0), (0, 0), (0, 0)]
    padding[along] = (16, 16)
    widened = jnp.pad(values, padding)
    summed = jnp.zeros_like(values)
    for shift_at in range(33):
        summed = summed + kernel[shift_at] * lax.slice_in_dim(widened, shift_at, shift_at + length, axis=along)
    return summed

def smooth(values, kernel):
    return taps_along(taps_along(taps_along(values, 0, kernel), 1, kernel), 2, kernel)

def cone_work(inputs):
    received, resp, tile_offsets, tile_fracs, groups, slots, stars_obs, stars_sig = inputs
    sample_at = slots[:, None] * NZ + tile_offsets
    lower = received[sample_at].astype(jnp.float32)
    upper = received[sample_at + 1].astype(jnp.float32)
    samples = ((1.0 - tile_fracs) * lower + tile_fracs * upper).astype(jnp.bfloat16)
    tile_pred = jnp.einsum('tks,tk->ts', resp.astype(jnp.float32), samples.astype(jnp.float32))
    predicted = jax.ops.segment_sum(tile_pred, groups, num_segments=G_DEV)
    resid = (predicted - stars_obs) / (stars_sig * stars_sig)
    tile_resid = resid[groups].astype(jnp.bfloat16)
    back = jnp.einsum('tks,ts->tk', resp.astype(jnp.float32), tile_resid.astype(jnp.float32))
    flat_grad = jnp.zeros((NDEV * CAP * NZ,), jnp.float32)
    flat_grad = flat_grad.at[sample_at].add((1.0 - tile_fracs) * back)
    flat_grad = flat_grad.at[sample_at + 1].add(tile_fracs * back)
    return (predicted.reshape(-1), flat_grad)

def owner_sum(inputs):
    grads, targets = inputs
    summed = jax.ops.segment_sum(grads.reshape(-1, NZ), targets.reshape(-1), num_segments=CXV * CYV + 1)
    return summed[:CXV * CYV]

def reference(latent, observed, sigma, response, offsets, fractions, tile_group, tile_slot, send_index):
    kernel = kernel_taps()
    density = jnp.exp(smooth(latent, kernel))
    columns = density.reshape(N_CX, CXV, N_CY, CYV, NZ).transpose(0, 2, 1, 3, 4).reshape(NDEV, CXV * CYV, NZ)
    sent = columns.astype(jnp.bfloat16)
    valid = send_index >= 0
    safe_rows = jnp.maximum(send_index, 0)
    packed = jax.vmap(lambda owned, rows: owned[rows])(sent, safe_rows)
    packed = jnp.where(valid[..., None], packed, jnp.zeros((), jnp.bfloat16))
    blocks = packed.transpose(1, 0, 2, 3).reshape(NDEV, NDEV * CAP * NZ)
    inputs = (blocks, response.reshape(NDEV, TILES_DEV, SAMPLES, STAR_TILE), offsets.reshape(SAMPLES, NDEV, TILES_DEV).transpose(1, 2, 0).astype(jnp.int32), fractions.reshape(SAMPLES, NDEV, TILES_DEV).transpose(1, 2, 0), tile_group.reshape(NDEV, TILES_DEV).astype(jnp.int32), tile_slot.reshape(NDEV, TILES_DEV).astype(jnp.int32), observed.reshape(NDEV, G_DEV, STAR_TILE), sigma.reshape(NDEV, G_DEV, STAR_TILE))
    predicted, slot_grad = lax.map(cone_work, inputs)
    by_source = slot_grad.reshape(NDEV, NDEV, CAP, NZ).transpose(1, 0, 2, 3)
    targets = jnp.where(valid, safe_rows, CXV * CYV).astype(jnp.int32)
    column_grad = lax.map(owner_sum, (by_source, targets))
    dens_grad = column_grad.reshape(N_CX, N_CY, CXV, CYV, NZ).transpose(0, 2, 1, 3, 4).reshape(NX, NY, NZ)
    gradient = latent + smooth(density * dens_grad, kernel)
    return (gradient, predicted.reshape(-1))
```

```python
import functools

import jax
import jax.numpy as jnp
import ml_dtypes
import numpy as np
from jax import lax
from jax.experimental import pallas as pl
from jax.experimental.pallas import tpu as pltpu
from jax.sharding import PartitionSpec as P

F32, BF16 = jnp.float32, jnp.bfloat16
MESH = pl.DeviceIdType.MESH
LANES = 128


def smoothing_tables(rows_x, rows_y, depth):
    shifts = np.arange(-16, 17).astype(np.float32)
    scaled = np.sqrt(np.float32(3.0)) * np.abs(shifts) / np.float32(8.0)
    raw = (np.float32(1.0) + scaled) * np.exp(-scaled)
    taps = np.float32(0.8) * raw / np.sqrt(np.sum(raw * raw))

    def band(length, start):
        shift = np.arange(length)[None, :] + start - np.arange(length)[:, None]
        inside = np.abs(shift) <= 16
        return np.where(inside, taps[np.clip(shift + 16, 0, 32)], 0).astype(np.float32)

    whole = [np.kron(band(rows_x, s), np.eye(rows_y)) for s in (0, -rows_x, rows_x)]
    whole += [np.kron(np.eye(rows_x), band(rows_y, s)) for s in (0, -rows_y, rows_y)]
    whole += [band(depth, 0)]
    parts = []
    for table in whole:
        table = table.astype(np.float32)
        high = table.astype(ml_dtypes.bfloat16)
        parts += [high, (table - high.astype(np.float32)).astype(ml_dtypes.bfloat16)]
    return np.stack(parts)


def dot(a, b):
    return lax.dot_general(a, b, (((1,), (0,)), ((), ())), preferred_element_type=F32)


def dot_t(a, b):
    return lax.dot_general(a, b, (((1,), (1,)), ((), ())), preferred_element_type=F32)


def split(x):
    high = x.astype(BF16)
    return high, (x - high.astype(F32)).astype(BF16)


def one_hot(a, b):
    return jnp.where(a == b, 1.0, 0.0).astype(BF16)


def kernel(
    ncx, ncy, cap,
    latent, observed, sigma, response, offsets, fractions, group, slot, send, tables,
    gradient, predicted,
    resp, tabs, halo_out, halo_in, a_out, a_in, b_out, b_in, c_out, c_in, d_out, d_in,
    index, weight, odup, block_of, tile_pred, tile_resid, tile_grad, hot_out, hot_back,
    hot_slot, density,
    resp_sem, tab_sem, halo_send, halo_recv, x_send, x_recv, y_send, y_recv,
):
    cx, cy = lax.axis_index("cx"), lax.axis_index("cy")
    tiles = slot.shape[1]
    slots = ncx * ncy * cap
    samples = offsets.shape[0]
    chunk_rows = resp.shape[0] // resp_sem.shape[0]

    tab_copy = pltpu.make_async_copy(tables, tabs, tab_sem)
    tab_copy.start()
    resp_copies = [
        pltpu.make_async_copy(
            response.at[pl.ds(i * chunk_rows, chunk_rows)],
            resp.at[pl.ds(i * chunk_rows, chunk_rows)],
            resp_sem.at[i],
        )
        for i in range(resp_sem.shape[0])
    ]
    for copy in resp_copies:
        copy.start()

    barrier = pltpu.get_barrier_semaphore()
    for k in range(1, ncx):
        pl.semaphore_signal(
            barrier, inc=1, device_id=(lax.rem(cx + k, ncx), cy), device_id_type=MESH
        )
    for k in range(1, ncy):
        pl.semaphore_signal(
            barrier, inc=1, device_id=(cx, lax.rem(cy + k, ncy)), device_id_type=MESH
        )
    halo_out[0] = latent[...].astype(BF16)
    pl.semaphore_wait(barrier, ncx + ncy - 2)

    def start_halo(at, along):
        copies = []
        for side in range(2):
            step = 1 if side == 0 else -1
            if along == "x":
                to = (lax.rem(cx + step + ncx, ncx), cy)
            else:
                to = (cx, lax.rem(cy + step + ncy, ncy))
            copy = pltpu.make_async_remote_copy(
                src_ref=halo_out.at[at],
                dst_ref=halo_in.at[2 * at + side],
                send_sem=halo_send.at[2 * at + side],
                recv_sem=halo_recv.at[2 * at + side],
                device_id=to,
                device_id_type=MESH,
            )
            copy.start()
            copies.append(copy)
        return copies

    def own_part(x, at):
        high, low = split(x)
        return (
            dot(tabs[2 * at], high) + dot(tabs[2 * at + 1], high) + dot(tabs[2 * at], low)
        )

    def halo_part(copies, at, first):
        place, count = (cx, ncx) if first == 0 else (cy, ncy)
        copies[0].wait_recv()
        copies[1].wait_recv()
        left = halo_in[2 * at]
        right = halo_in[2 * at + 1]
        from_left = dot(tabs[2 * first + 2], left) + dot(tabs[2 * first + 3], left)
        from_right = dot(tabs[2 * first + 4], right) + dot(tabs[2 * first + 5], right)
        zero = jnp.zeros_like(from_left)
        return jnp.where(place > 0, from_left, zero) + jnp.where(
            place < count - 1, from_right, zero
        )

    def along_z(x):
        high, low = split(x)
        return dot(high, tabs[12]) + dot(high, tabs[13]) + dot(low, tabs[12])

    def swap(out, into, along):
        count, me = (ncx, cx) if along == "x" else (ncy, cy)
        send_sem, recv_sem = (x_send, x_recv) if along == "x" else (y_send, y_recv)
        at = 0 if (into is a_in or into is b_in) else 1
        copies = []
        for k in range(1, count):
            to = lax.rem(me + k, count)
            copy = pltpu.make_async_remote_copy(
                src_ref=out.at[to],
                dst_ref=into.at[me],
                send_sem=send_sem.at[at * count + k],
                recv_sem=recv_sem.at[at * count + k],
                device_id=(to, cy) if along == "x" else (cx, to),
                device_id_type=MESH,
            )
            copy.start()
            copies.append(copy)
        into[me] = out[me]
        return copies

    started = []
    copies = start_halo(0, "x")
    started += copies

    def columns_of(row):
        return jnp.broadcast_to(row.astype(F32), (LANES, row.shape[1])).T

    lane_of = lax.broadcasted_iota(jnp.int32, (1, LANES), 1).astype(F32)
    voxels = latent.shape[0]
    depth = latent.shape[1]
    send_col = columns_of(send[...])
    for j in range(voxels // LANES):
        hot_out[:, j * LANES : (j + 1) * LANES] = one_hot(send_col, lane_of + j * LANES)
    row_of = lax.broadcasted_iota(jnp.int32, (voxels, 1), 0).astype(F32)
    hot_back[...] = one_hot(row_of, send[...].astype(F32))
    q = slot[...]
    per_x = ncy * cap
    place = (lax.rem(q, per_x) // cap) * (ncx * cap) + (q // per_x) * cap + lax.rem(q, cap)
    place_row = place.astype(F32)
    slot_row = lax.broadcasted_iota(jnp.int32, (slots, 1), 0).astype(F32)
    hot_slot[...] = one_hot(slot_row, place_row)
    below = offsets[...].astype(F32)
    index[...] = jnp.concatenate([below, below + 1.0], axis=0).T.astype(jnp.int32)
    odup[...] = jnp.concatenate([below, below], axis=0).T
    share = fractions[...]
    weight[...] = jnp.concatenate([1.0 - share, share], axis=0).T

    tab_copy.wait()
    field = own_part(latent[...], 0)
    field = field + halo_part(copies, 0, 0)
    halo_out[1] = field.astype(BF16)
    copies = start_halo(1, "y")
    started += copies
    field = own_part(field, 3) + halo_part(copies, 1, 3)
    dens = jnp.exp(along_z(field))
    density[...] = dens

    packed = dot(hot_out[...], dens.astype(BF16)).astype(BF16)
    a_out[...] = packed.reshape(a_out.shape)
    copies = swap(a_out, a_in, "x")
    started += copies
    to_y = lax.broadcasted_iota(jnp.int32, (slots, 1), 0)
    wanted = (
        (lax.rem(to_y, ncx * cap) // cap) * per_x
        + (to_y // (ncx * cap)) * cap
        + lax.rem(to_y, cap)
    ).astype(F32)
    all_slots = lax.broadcasted_iota(jnp.int32, (1, slots), 1).astype(F32)
    turn = one_hot(wanted, all_slots)
    for copy in copies:
        copy.wait_recv()
    b_out[...] = dot(turn, a_in[...].reshape(slots, depth)).astype(BF16).reshape(b_out.shape)
    copies = swap(b_out, b_in, "y")
    started += copies
    place_col = columns_of(place)
    hot_tile = jnp.concatenate(
        [one_hot(place_col, lane_of + j * LANES) for j in range(-(-slots // LANES))], axis=1
    )[:, :slots]
    for copy in copies:
        copy.wait_recv()
    block_of[...] = dot(hot_tile, b_in[...].reshape(slots, depth))

    for copy in resp_copies:
        copy.wait()
    pair_of = lax.broadcasted_iota(jnp.int32, (8, LANES), 0) // 2
    odd_row = lax.rem(lax.broadcasted_iota(jnp.int32, (8, LANES), 0), 2)
    upper = lax.broadcasted_iota(jnp.int32, (8, LANES), 1) // samples
    masks = [
        jnp.where((pair_of == j) & (odd_row == upper), 1.0, 0.0) for j in range(4)
    ]
    high_lane = lax.broadcasted_iota(jnp.int32, (8, LANES), 1) >= samples

    def forward(g, carry):
        rows = pl.ds(pl.multiple_of(g * 8, 8), 8)
        at = index[rows, :]
        near = at & (LANES - 1)
        low = jnp.take_along_axis(
            block_of[rows, 0:LANES], near, axis=1, mode="promise_in_bounds"
        )
        far = jnp.take_along_axis(
            block_of[rows, LANES : 2 * LANES], near, axis=1, mode="promise_in_bounds"
        )
        terms = jnp.where(at < LANES, low, far) * weight[rows, :]
        sample = (terms + pltpu.roll(terms, samples, 1)).astype(BF16).astype(F32)
        left = jnp.concatenate([sample * m for m in masks], axis=1).astype(BF16)
        tile_pred[rows, :] = dot(left, resp[pl.ds(pl.multiple_of(g * 512, 512), 512), :])
        return carry

    lax.fori_loop(0, tiles // 8, forward, 0, unroll=4)

    groups = observed.shape[0]
    group_row = group[...].astype(F32)
    group_of = lax.broadcasted_iota(jnp.int32, (groups, 1), 0).astype(F32)
    hot_group = one_hot(group_of, group_row)
    high, low = split(tile_pred[...])
    total = dot(hot_group, high) + dot(hot_group, low)
    predicted[...] = total
    resid = (total - observed[...]) / (sigma[...] * sigma[...])
    resid = jnp.concatenate([resid, jnp.zeros((LANES - groups, LANES), F32)], axis=0)
    hot_of_tile = one_hot(columns_of(group[...]), lane_of)
    tile_resid[...] = dot(hot_of_tile, resid.astype(BF16))

    dist = lax.broadcasted_iota(jnp.int32, (depth, 1), 0).astype(F32)
    masks2 = [jnp.concatenate([m, m], axis=0) for m in masks]

    def backward(g, carry):
        rows = pl.ds(pl.multiple_of(g * 8, 8), 8)
        back = dot_t(
            tile_resid[rows, :].astype(BF16),
            resp[pl.ds(pl.multiple_of(g * 512, 512), 512), :],
        )
        own = sum(back[:, j * LANES : (j + 1) * LANES] * masks[j] for j in range(4))
        own = own + pltpu.roll(own, samples, 1)
        parts = own * weight[rows, :]
        turned = pltpu.roll(parts, samples, 1)
        both = jnp.concatenate(
            [jnp.where(high_lane, turned, parts), jnp.where(high_lane, parts, turned)], axis=0
        )
        high = both.astype(BF16).astype(F32)
        low = both - high
        left = jnp.concatenate(
            [
                jnp.concatenate([high * m for m in masks2], axis=1).astype(BF16),
                jnp.concatenate([low * m for m in masks2], axis=1).astype(BF16),
            ],
            axis=0,
        )
        even = odup[rows, :]
        hot = []
        for j in range(4):
            at = jnp.where(high_lane[0:1], even[2 * j + 1 : 2 * j + 2], even[2 * j : 2 * j + 1])
            hot.append(one_hot(dist, at))
        out = dot_t(left, jnp.concatenate(hot, axis=1))
        lower = out[0:8] + out[16:24]
        raised = out[8:16] + out[24:32]
        tile_grad[rows, :] = lower + pltpu.roll(raised, 1, 1)
        return carry

    lax.fori_loop(0, tiles // 8, backward, 0, unroll=4)

    high, low = split(tile_grad[...])
    slot_grad = dot(hot_slot[...], high) + dot(hot_slot[...], low)

    c_out[...] = slot_grad.astype(BF16).reshape(c_out.shape)
    copies = swap(c_out, c_in, "y")
    started += copies
    wanted = (
        (lax.rem(to_y, per_x) // cap) * (ncx * cap) + (to_y // per_x) * cap + lax.rem(to_y, cap)
    ).astype(F32)
    turn = one_hot(wanted, all_slots)
    for copy in copies:
        copy.wait_recv()
    d_out[...] = dot(turn, c_in[...].reshape(slots, depth)).astype(BF16).reshape(d_out.shape)
    copies = swap(d_out, d_in, "x")
    started += copies
    for copy in copies:
        copy.wait_recv()
    dens_grad = dot(hot_back[...], d_in[...].reshape(slots, depth))

    field = density[...] * dens_grad
    halo_out[2] = field.astype(BF16)
    copies = start_halo(2, "x")
    started += copies
    field = own_part(field, 0) + halo_part(copies, 2, 0)
    halo_out[3] = field.astype(BF16)
    copies = start_halo(3, "y")
    started += copies
    field = own_part(field, 3) + halo_part(copies, 3, 3)
    gradient[...] = latent[...] + along_z(field)
    for copy in started:
        copy.wait_send()


def on_device(
    latent, observed, sigma, response, offsets, fractions, tile_group, tile_slot, send_index
):
    ncx, ncy = lax.axis_size("cx"), lax.axis_size("cy")
    rows_x, rows_y, depth = latent.shape
    tiles, samples, star_tile = response.shape
    groups = observed.shape[0] // star_tile
    cap = send_index.shape[2]
    voxels = rows_x * rows_y
    slots = ncx * ncy * cap
    tables = smoothing_tables(rows_x, rows_y, depth)
    chunks = 4
    vmem = pl.BlockSpec(memory_space=pltpu.VMEM)
    anywhere = pl.BlockSpec(memory_space=pl.ANY)
    gradient, predicted = pl.pallas_call(
        functools.partial(kernel, ncx, ncy, cap),
        out_shape=(
            jax.ShapeDtypeStruct((voxels, depth), F32),
            jax.ShapeDtypeStruct((groups, star_tile), F32),
        ),
        in_specs=[vmem, vmem, vmem, anywhere, vmem, vmem, vmem, vmem, vmem, anywhere],
        out_specs=(vmem, vmem),
        scratch_shapes=[
            pltpu.VMEM((tiles * samples, star_tile), BF16),
            pltpu.VMEM(tables.shape, BF16),
            pltpu.VMEM((4, voxels, depth), BF16),
            pltpu.VMEM((8, voxels, depth), BF16),
            pltpu.VMEM((ncx, ncy * cap, depth), BF16),
            pltpu.VMEM((ncx, ncy * cap, depth), BF16),
            pltpu.VMEM((ncy, ncx * cap, depth), BF16),
            pltpu.VMEM((ncy, ncx * cap, depth), BF16),
            pltpu.VMEM((ncy, ncx * cap, depth), BF16),
            pltpu.VMEM((ncy, ncx * cap, depth), BF16),
            pltpu.VMEM((ncx, ncy * cap, depth), BF16),
            pltpu.VMEM((ncx, ncy * cap, depth), BF16),
            pltpu.VMEM((tiles, 2 * samples), jnp.int32),
            pltpu.VMEM((tiles, 2 * samples), F32),
            pltpu.VMEM((tiles, 2 * samples), F32),
            pltpu.VMEM((tiles, depth), F32),
            pltpu.VMEM((tiles, star_tile), F32),
            pltpu.VMEM((tiles, star_tile), F32),
            pltpu.VMEM((tiles, depth), F32),
            pltpu.VMEM((slots, voxels), BF16),
            pltpu.VMEM((voxels, slots), BF16),
            pltpu.VMEM((slots, tiles), BF16),
            pltpu.VMEM((voxels, depth), F32),
            pltpu.SemaphoreType.DMA((chunks,)),
            pltpu.SemaphoreType.DMA,
            pltpu.SemaphoreType.DMA((8,)),
            pltpu.SemaphoreType.DMA((8,)),
            pltpu.SemaphoreType.DMA((2 * ncx,)),
            pltpu.SemaphoreType.DMA((2 * ncx,)),
            pltpu.SemaphoreType.DMA((2 * ncy,)),
            pltpu.SemaphoreType.DMA((2 * ncy,)),
        ],
        compiler_params=pltpu.CompilerParams(
            collective_id=0, has_side_effects=True, vmem_limit_bytes=48 * 1024 * 1024
        ),
        name="dust_map",
    )(
        latent.reshape(voxels, depth),
        observed.reshape(groups, star_tile),
        sigma.reshape(groups, star_tile),
        response.reshape(tiles * samples, star_tile),
        offsets,
        fractions,
        tile_group.reshape(1, tiles),
        tile_slot.reshape(1, tiles),
        send_index.reshape(1, slots),
        jnp.asarray(tables),
    )
    return gradient.reshape(latent.shape), predicted.reshape(-1)


def solution(mesh):
    placed = (
        P("cx", "cy", None),
        P(("cx", "cy")),
        P(("cx", "cy")),
        P(("cx", "cy"), None, None),
        P(None, ("cx", "cy")),
        P(None, ("cx", "cy")),
        P(("cx", "cy")),
        P(("cx", "cy")),
        P(("cx", "cy"), None, None),
    )
    return jax.shard_map(
        on_device,
        mesh=mesh,
        in_specs=placed,
        out_specs=(P("cx", "cy", None), P(("cx", "cy"))),
        check_vma=False,
    )
```

```python
import functools

import jax
import jax.numpy as jnp
import ml_dtypes
import numpy as np
from jax import lax
from jax.experimental import pallas as pl
from jax.experimental.pallas import tpu as pltpu
from jax.sharding import PartitionSpec as P

F32, BF16 = jnp.float32, jnp.bfloat16
MESH = pl.DeviceIdType.MESH
LANES = 128
UNROLL_SENDS = 8
SET = 16
CHUNKS_X, CHUNKS_Y, CHUNKS_SWAP = (0, 1), (2, 3, 4), (5, 6, 7)


def smoothing_tables(rows_x, rows_y, depth):
    shifts = np.arange(-16, 17).astype(np.float32)
    scaled = np.sqrt(np.float32(3.0)) * np.abs(shifts) / np.float32(8.0)
    raw = (np.float32(1.0) + scaled) * np.exp(-scaled)
    taps = np.float32(0.8) * raw / np.sqrt(np.sum(raw * raw))

    def band(length, start):
        shift = np.arange(length)[None, :] + start - np.arange(length)[:, None]
        inside = np.abs(shift) <= 16
        return np.where(inside, taps[np.clip(shift + 16, 0, 32)], 0).astype(np.float32)

    whole = [np.kron(band(rows_x, s), np.eye(rows_y)) for s in (0, -rows_x, rows_x)]
    whole += [np.kron(np.eye(rows_x), band(rows_y, s)) for s in (0, -rows_y, rows_y)]
    whole += [band(depth, 0)]
    parts = []
    for table in whole:
        table = table.astype(np.float32)
        high = table.astype(ml_dtypes.bfloat16)
        parts += [high, (table - high.astype(np.float32)).astype(ml_dtypes.bfloat16)]
    return np.stack(parts)


def dot(a, b):
    return lax.dot_general(a, b, (((1,), (0,)), ((), ())), preferred_element_type=F32)


def dot_t(a, b):
    return lax.dot_general(a, b, (((1,), (1,)), ((), ())), preferred_element_type=F32)


def split(x):
    high = x.astype(BF16)
    return high, (x - high.astype(F32)).astype(BF16)


def one_hot(a, b):
    return jnp.where(a == b, 1.0, 0.0).astype(BF16)


def kernel(
    ncx, ncy, cap,
    latent_hbm, observed_hbm, sigma_hbm, response, offsets_hbm, fractions_hbm, group_hbm,
    slot_hbm, send_hbm, tables,
    gradient, predicted,
    latent, observed, sigma, offsets, fractions, group, slot, send, resp, resp_t, hot_near, tabs,
    halo_out, halo_in, there_out, there_in, back_out, back_in,
    index, weight, odup, low_index, block_of, tile_pred, tile_resid, tile_grad,
    hot_out, hot_back, hot_slot, density,
    in_sem, resp_sem, tab_sem, halo_send, halo_recv, swap_send, swap_recv, ready,
):
    cx, cy = lax.axis_index("cx"), lax.axis_index("cy")
    tiles = slot.shape[1]
    slots = ncx * ncy * cap
    samples = offsets.shape[0]
    chunk_rows = resp.shape[0] // resp_sem.shape[0]

    in_copies = [
        pltpu.make_async_copy(source, target, in_sem.at[i])
        for i, (source, target) in enumerate(
            [
                (latent_hbm, latent),
                (send_hbm, send),
                (slot_hbm, slot),
                (offsets_hbm, offsets),
                (fractions_hbm, fractions),
                (group_hbm, group),
                (observed_hbm, observed),
                (sigma_hbm, sigma),
            ]
        )
    ]
    for copy in in_copies:
        copy.start()
    tab_copy = pltpu.make_async_copy(tables, tabs, tab_sem)
    tab_copy.start()
    resp_copies = [
        pltpu.make_async_copy(
            response.at[pl.ds(i * chunk_rows, chunk_rows)],
            resp.at[pl.ds(i * chunk_rows, chunk_rows)],
            resp_sem.at[i],
        )
        for i in range(resp_sem.shape[0])
    ]
    for copy in resp_copies:
        copy.start()

    barrier = pltpu.get_barrier_semaphore()
    for k in range(1, ncx):
        pl.semaphore_signal(
            barrier, inc=1, device_id=(lax.rem(cx + k, ncx), cy), device_id_type=MESH
        )
    for k in range(1, ncy):
        pl.semaphore_signal(
            barrier, inc=1, device_id=(cx, lax.rem(cy + k, ncy)), device_id_type=MESH
        )
    in_copies[0].wait()
    halo_out[0] = latent[...].astype(BF16)
    pl.semaphore_wait(barrier, ncx + ncy - 2)
    for k in range(1, ncx):
        pl.semaphore_signal(
            ready, inc=1, device_id=(lax.rem(cx + k, ncx), cy), device_id_type=MESH
        )

    def start_halo(at, along):
        copies = []
        for side in range(2):
            step = 1 if side == 0 else -1
            if along == "x":
                to = (lax.rem(cx + step + ncx, ncx), cy)
            else:
                to = (cx, lax.rem(cy + step + ncy, ncy))
            copy = pltpu.make_async_remote_copy(
                src_ref=halo_out.at[at],
                dst_ref=halo_in.at[2 * at + side],
                send_sem=halo_send.at[2 * at + side],
                recv_sem=halo_recv.at[2 * at + side],
                device_id=to,
                device_id_type=MESH,
            )
            copy.start()
            copies.append(copy)
        return copies

    def own_part(x, at):
        high, low = split(x)
        return (
            dot(tabs[2 * at], high) + dot(tabs[2 * at + 1], high) + dot(tabs[2 * at], low)
        )

    def halo_part(copies, at, first):
        place, count = (cx, ncx) if first == 0 else (cy, ncy)
        copies[0].wait_recv()
        copies[1].wait_recv()
        left = halo_in[2 * at]
        right = halo_in[2 * at + 1]
        from_left = dot(tabs[2 * first + 2], left) + dot(tabs[2 * first + 3], left)
        from_right = dot(tabs[2 * first + 4], right) + dot(tabs[2 * first + 5], right)
        zero = jnp.zeros_like(from_left)
        return jnp.where(place > 0, from_left, zero) + jnp.where(
            place < count - 1, from_right, zero
        )

    def along_z(x):
        high, low = split(x)
        return dot(high, tabs[12]) + dot(high, tabs[13]) + dot(low, tabs[12])

    count = ncx * ncy
    me = cx * ncy + cy

    def start_swap(out, into, at):
        def send_to(k, carry):
            to = lax.rem(me + k, count)
            pltpu.make_async_remote_copy(
                src_ref=out.at[to],
                dst_ref=into.at[me],
                send_sem=swap_send.at[at],
                recv_sem=swap_recv.at[at],
                device_id=(to // ncy, lax.rem(to, ncy)),
                device_id_type=MESH,
            ).start()
            return carry

        lax.fori_loop(1, count, send_to, 0, unroll=UNROLL_SENDS)
        into[me] = out[me]

    def all_but_one(ref, sem):
        part = ref.at[pl.ds(0, count - 1)]
        return pltpu.make_async_copy(part, part, sem)

    started = []
    copies = start_halo(0, "x")
    started += copies

    for copy in in_copies[1:]:
        copy.wait()

    def columns_of(row):
        return jnp.broadcast_to(row.astype(F32), (LANES, row.shape[1])).T

    lane_of = lax.broadcasted_iota(jnp.int32, (1, LANES), 1).astype(F32)
    voxels = latent.shape[0]
    depth = latent.shape[1]
    send_col = columns_of(send[...])
    for j in range(voxels // LANES):
        hot_out[:, j * LANES : (j + 1) * LANES] = one_hot(send_col, lane_of + j * LANES)
    row_of = lax.broadcasted_iota(jnp.int32, (voxels, 1), 0).astype(F32)
    hot_back[...] = one_hot(row_of, send[...].astype(F32))
    slot_row = lax.broadcasted_iota(jnp.int32, (slots, 1), 0).astype(F32)
    hot_slot[...] = one_hot(slot_row, slot[...].astype(F32))
    below = offsets[...].astype(F32)
    index[...] = jnp.concatenate([below, below + 1.0], axis=0).T.astype(jnp.int32)
    odup[...] = jnp.concatenate([below, below], axis=0).T
    share = fractions[...]
    weight[...] = jnp.concatenate([1.0 - share, share], axis=0).T
    low_index[...] = jnp.where(below >= LANES, below - LANES, below)
    group_rows = 8 * samples

    def prepare(g, carry):
        rows = pl.ds(pl.multiple_of(g * group_rows, group_rows), group_rows)
        resp_t[g] = resp[rows, :].T
        first = g * 8
        strip = low_index[:, pl.ds(pl.multiple_of(first // LANES * LANES, LANES), LANES)]
        hots = []
        for t in range(8):
            lane = jnp.full((samples, LANES), lax.rem(first, LANES) + t, jnp.int32)
            at = jnp.take_along_axis(strip, lane, axis=1, mode="promise_in_bounds")
            hots.append(one_hot(at, lane_of))
        hot_near[rows, :] = jnp.concatenate(hots, axis=0)
        return carry

    steps = tiles // 8
    per_chunk = steps // len(resp_copies)

    def prepare_chunks(chunks):
        for i in chunks:
            resp_copies[i].wait()
            lax.fori_loop(i * per_chunk, (i + 1) * per_chunk, prepare, 0, unroll=4)


    tab_copy.wait()
    field = own_part(latent[...], 0)
    prepare_chunks(CHUNKS_X)
    field = field + halo_part(copies, 0, 0)
    halo_out[1] = field.astype(BF16)
    copies = start_halo(1, "y")
    started += copies
    field = own_part(field, 3)
    prepare_chunks(CHUNKS_Y)
    field = field + halo_part(copies, 1, 3)
    dens = jnp.exp(along_z(field))
    density[...] = dens

    packed = dot(hot_out[...], dens.astype(BF16)).astype(BF16)
    there_out[...] = packed.reshape(there_out.shape)
    pl.semaphore_wait(ready, ncx - 1)
    start_swap(there_out, there_in, 0)
    prepare_chunks(CHUNKS_SWAP)
    slot_col = columns_of(slot[...])
    hot_tile = jnp.concatenate(
        [one_hot(slot_col, lane_of + j * LANES) for j in range(-(-slots // LANES))], axis=1
    )[:, :slots]
    all_but_one(there_in, swap_recv.at[0]).wait()
    block_of[...] = dot(hot_tile, there_in[...].reshape(slots, depth))

    pair_of = lax.broadcasted_iota(jnp.int32, (8, LANES), 0) // 2
    odd_row = lax.rem(lax.broadcasted_iota(jnp.int32, (8, LANES), 0), 2)
    upper = lax.broadcasted_iota(jnp.int32, (8, LANES), 1) // samples
    keep = [(pair_of == j) & (odd_row == upper) for j in range(4)]
    masks = [jnp.where(k, 1.0, 0.0) for k in keep]
    high_lane = lax.broadcasted_iota(jnp.int32, (1, LANES), 1) >= samples
    masks = [m.astype(BF16) for m in masks]
    set_of = 8 * SET

    def forward(i, carry):
        first = pl.multiple_of(i * set_of, set_of)
        rows = pl.ds(first, set_of)
        at = index[rows, :]
        near = at & (LANES - 1)
        low = jnp.take_along_axis(
            block_of[rows, 0:LANES], near, axis=1, mode="promise_in_bounds"
        )
        far = jnp.take_along_axis(
            block_of[rows, LANES : 2 * LANES], near, axis=1, mode="promise_in_bounds"
        )
        terms = jnp.where(at < LANES, low, far) * weight[rows, :]
        sample = (terms + pltpu.roll(terms, samples, 1)).astype(BF16)
        lefts = []
        for j in range(SET):
            own = sample[8 * j : 8 * j + 8]
            lefts.append(jnp.concatenate([own * m for m in masks], axis=1))
        preds = []
        for j in range(SET):
            at_row = pl.multiple_of(first * samples + j * group_rows, group_rows)
            preds.append(dot(lefts[j], resp[pl.ds(at_row, group_rows), :]))
        tile_pred[rows, :] = jnp.concatenate(preds, axis=0)
        return carry

    lax.fori_loop(0, tiles // set_of, forward, 0)

    groups = observed.shape[0]
    group_row = group[...].astype(F32)
    group_of = lax.broadcasted_iota(jnp.int32, (groups, 1), 0).astype(F32)
    hot_group = one_hot(group_of, group_row)
    high, low = split(tile_pred[...])
    total = dot(hot_group, high) + dot(hot_group, low)
    predicted[...] = total
    resid = (total - observed[...]) / (sigma[...] * sigma[...])
    resid = jnp.concatenate([resid, jnp.zeros((LANES - groups, LANES), F32)], axis=0)
    hot_of_tile = one_hot(columns_of(group[...]), lane_of)
    tile_resid[...] = dot(hot_of_tile, resid.astype(BF16))

    masks2 = [jnp.concatenate([m, m], axis=0) for m in masks]

    def backward(i, carry):
        first = pl.multiple_of(i * set_of, set_of)
        rows = pl.ds(first, set_of)
        tr = tile_resid[rows, :].astype(BF16)
        backs = [dot(tr[8 * j : 8 * j + 8], resp_t[i * SET + j]) for j in range(SET)]
        own = jnp.concatenate(
            [
                sum(
                    jnp.where(keep[n], back[:, n * LANES : (n + 1) * LANES], 0.0)
                    for n in range(4)
                )
                for back in backs
            ],
            axis=0,
        )
        own = own + pltpu.roll(own, samples, 1)
        parts = own * weight[rows, :]
        turned = pltpu.roll(parts, samples, 1)
        v_low = jnp.where(high_lane, turned, parts)
        v_high = jnp.where(high_lane, parts, turned)
        is_far = odup[rows, :] >= LANES
        kinds = [
            jnp.where(is_far, 0.0, v_low),
            jnp.where(is_far, 0.0, v_high),
            jnp.where(is_far, v_low, 0.0),
            jnp.where(is_far, v_high, 0.0),
        ]
        lefts = []
        for j in range(SET):
            own_kinds = [kind[8 * j : 8 * j + 8] for kind in kinds]
            near = jnp.concatenate(own_kinds[0:2], axis=0).astype(BF16)
            far = jnp.concatenate(own_kinds[2:4], axis=0).astype(BF16)
            lefts.append(
                jnp.concatenate(
                    [
                        jnp.concatenate([near * m for m in masks2], axis=1),
                        jnp.concatenate([far * m for m in masks2], axis=1),
                    ],
                    axis=0,
                )
            )
        outs = []
        for j in range(SET):
            at_row = pl.multiple_of(first * samples + j * group_rows, group_rows)
            outs.append(dot(lefts[j], hot_near[pl.ds(at_row, group_rows), :]))
        lower_near = jnp.concatenate([out[0:8] for out in outs], axis=0)
        raised_near = jnp.concatenate([out[8:16] for out in outs], axis=0)
        lower_far = jnp.concatenate([out[16:24] for out in outs], axis=0)
        raised_far = jnp.concatenate([out[24:32] for out in outs], axis=0)
        raised = jnp.concatenate([raised_near, raised_far], axis=1)
        lower = jnp.concatenate([lower_near, lower_far], axis=1)
        tile_grad[rows, :] = lower + pltpu.roll(raised, 1, 1)
        return carry

    lax.fori_loop(0, tiles // set_of, backward, 0)

    high, low = split(tile_grad[...])
    slot_grad = dot(hot_slot[...], high) + dot(hot_slot[...], low)

    back_out[...] = slot_grad.astype(BF16).reshape(back_out.shape)
    start_swap(back_out, back_in, 1)
    all_but_one(back_in, swap_recv.at[1]).wait()
    dens_grad = dot(hot_back[...], back_in[...].reshape(slots, depth))

    field = density[...] * dens_grad
    halo_out[2] = field.astype(BF16)
    copies = start_halo(2, "x")
    started += copies
    field = own_part(field, 0) + halo_part(copies, 2, 0)
    halo_out[3] = field.astype(BF16)
    copies = start_halo(3, "y")
    started += copies
    field = own_part(field, 3) + halo_part(copies, 3, 3)
    gradient[...] = latent[...] + along_z(field)
    for copy in started:
        copy.wait_send()
    all_but_one(there_out, swap_send.at[0]).wait()
    all_but_one(back_out, swap_send.at[1]).wait()


def on_device(
    latent, observed, sigma, response, offsets, fractions, tile_group, tile_slot, send_index
):
    ncx, ncy = lax.axis_size("cx"), lax.axis_size("cy")
    rows_x, rows_y, depth = latent.shape
    tiles, samples, star_tile = response.shape
    groups = observed.shape[0] // star_tile
    cap = send_index.shape[2]
    voxels = rows_x * rows_y
    slots = ncx * ncy * cap
    tables = smoothing_tables(rows_x, rows_y, depth)
    chunks = 8
    vmem = pl.BlockSpec(memory_space=pltpu.VMEM)
    anywhere = pl.BlockSpec(memory_space=pltpu.HBM)
    gradient, predicted = pl.pallas_call(
        functools.partial(kernel, ncx, ncy, cap),
        out_shape=(
            jax.ShapeDtypeStruct((voxels, depth), F32),
            jax.ShapeDtypeStruct((groups, star_tile), F32),
        ),
        in_specs=[anywhere] * 10,
        out_specs=(vmem, vmem),
        scratch_shapes=[
            pltpu.VMEM((voxels, depth), F32),
            pltpu.VMEM((groups, star_tile), F32),
            pltpu.VMEM((groups, star_tile), F32),
            pltpu.VMEM((samples, tiles), jnp.int32),
            pltpu.VMEM((samples, tiles), F32),
            pltpu.VMEM((1, tiles), jnp.int32),
            pltpu.VMEM((1, tiles), jnp.int32),
            pltpu.VMEM((1, slots), jnp.int32),
            pltpu.VMEM((tiles * samples, star_tile), BF16),
            pltpu.VMEM((tiles // 8, star_tile, 8 * samples), BF16),
            pltpu.VMEM((tiles * samples, LANES), BF16),
            pltpu.VMEM(tables.shape, BF16),
            pltpu.VMEM((4, voxels, depth), BF16),
            pltpu.VMEM((8, voxels, depth), BF16),
            pltpu.VMEM((ncx * ncy, cap, depth), BF16),
            pltpu.VMEM((ncx * ncy, cap, depth), BF16),
            pltpu.VMEM((ncx * ncy, cap, depth), BF16),
            pltpu.VMEM((ncx * ncy, cap, depth), BF16),
            pltpu.VMEM((tiles, 2 * samples), jnp.int32),
            pltpu.VMEM((tiles, 2 * samples), F32),
            pltpu.VMEM((tiles, 2 * samples), F32),
            pltpu.VMEM((samples, tiles), F32),
            pltpu.VMEM((tiles, depth), F32),
            pltpu.VMEM((tiles, star_tile), F32),
            pltpu.VMEM((tiles, star_tile), F32),
            pltpu.VMEM((tiles, depth), F32),
            pltpu.VMEM((slots, voxels), BF16),
            pltpu.VMEM((voxels, slots), BF16),
            pltpu.VMEM((slots, tiles), BF16),
            pltpu.VMEM((voxels, depth), F32),
            pltpu.SemaphoreType.DMA((8,)),
            pltpu.SemaphoreType.DMA((chunks,)),
            pltpu.SemaphoreType.DMA,
            pltpu.SemaphoreType.DMA((8,)),
            pltpu.SemaphoreType.DMA((8,)),
            pltpu.SemaphoreType.DMA((2,)),
            pltpu.SemaphoreType.DMA((2,)),
            pltpu.SemaphoreType.REGULAR,
        ],
        compiler_params=pltpu.CompilerParams(
            collective_id=0, has_side_effects=True, vmem_limit_bytes=62 * 1024 * 1024
        ),
        name="dust_map",
    )(
        latent.reshape(voxels, depth),
        observed.reshape(groups, star_tile),
        sigma.reshape(groups, star_tile),
        response.reshape(tiles * samples, star_tile),
        offsets,
        fractions,
        tile_group.reshape(1, tiles),
        tile_slot.reshape(1, tiles),
        send_index.reshape(1, slots),
        jnp.asarray(tables),
    )
    return gradient.reshape(latent.shape), predicted.reshape(-1)


def solution(mesh):
    placed = (
        P("cx", "cy", None),
        P(("cx", "cy")),
        P(("cx", "cy")),
        P(("cx", "cy"), None, None),
        P(None, ("cx", "cy")),
        P(None, ("cx", "cy")),
        P(("cx", "cy")),
        P(("cx", "cy")),
        P(("cx", "cy"), None, None),
    )
    return jax.shard_map(
        on_device,
        mesh=mesh,
        in_specs=placed,
        out_specs=(P("cx", "cy", None), P(("cx", "cy"))),
        check_vma=False,
    )
```

```python
import functools

import jax
import jax.numpy as jnp
import ml_dtypes
import numpy as np
from jax import lax
from jax.experimental import pallas as pl
from jax.experimental.pallas import tpu as pltpu
from jax.sharding import PartitionSpec as P

F32, BF16 = jnp.float32, jnp.bfloat16
MESH = pl.DeviceIdType.MESH
LANES = 128
UNROLL_SENDS = 8
SET = 32
CHUNKS_X, CHUNKS_Y, CHUNKS_SWAP = (0, 1), (2, 3, 4), (5, 6, 7)


def smoothing_tables(rows_x, rows_y, depth):
    shifts = np.arange(-16, 17).astype(np.float32)
    scaled = np.sqrt(np.float32(3.0)) * np.abs(shifts) / np.float32(8.0)
    raw = (np.float32(1.0) + scaled) * np.exp(-scaled)
    taps = np.float32(0.8) * raw / np.sqrt(np.sum(raw * raw))

    def band(length, start):
        shift = np.arange(length)[None, :] + start - np.arange(length)[:, None]
        inside = np.abs(shift) <= 16
        return np.where(inside, taps[np.clip(shift + 16, 0, 32)], 0).astype(np.float32)

    whole = [np.kron(band(rows_x, s), np.eye(rows_y)) for s in (0, -rows_x, rows_x)]
    whole += [np.kron(np.eye(rows_x), band(rows_y, s)) for s in (0, -rows_y, rows_y)]
    whole += [band(depth, 0)]
    parts = []
    for table in whole:
        table = table.astype(np.float32)
        high = table.astype(ml_dtypes.bfloat16)
        parts += [high, (table - high.astype(np.float32)).astype(ml_dtypes.bfloat16)]
    return np.stack(parts)


def dot(a, b):
    return lax.dot_general(a, b, (((1,), (0,)), ((), ())), preferred_element_type=F32)


def dot_t(a, b):
    return lax.dot_general(a, b, (((1,), (1,)), ((), ())), preferred_element_type=F32)


def split(x):
    high = x.astype(BF16)
    return high, (x - high.astype(F32)).astype(BF16)


def one_hot(a, b):
    return jnp.where(a == b, 1.0, 0.0).astype(BF16)


def kernel(
    ncx, ncy, cap,
    latent_hbm, observed_hbm, sigma_hbm, response, offsets_hbm, fractions_hbm, group_hbm,
    slot_hbm, send_hbm, tables,
    gradient, predicted,
    latent, observed, sigma, offsets, fractions, group, slot, send, resp, resp_t, hot_near, tabs,
    halo_out, halo_in, there_out, there_in, back_out, back_in,
    index, weight, odup, low_index, block_of, tile_pred, tile_resid, tile_grad,
    hot_out, hot_back, hot_slot, hot_group, hot_of_tile, density,
    in_sem, resp_sem, tab_sem, halo_send, halo_recv, swap_send, swap_recv, ready,
):
    cx, cy = lax.axis_index("cx"), lax.axis_index("cy")
    tiles = slot.shape[1]
    slots = ncx * ncy * cap
    samples = offsets.shape[0]
    chunk_rows = resp.shape[0] // resp_sem.shape[0]

    in_copies = [
        pltpu.make_async_copy(source, target, in_sem.at[i])
        for i, (source, target) in enumerate(
            [
                (latent_hbm, latent),
                (send_hbm, send),
                (slot_hbm, slot),
                (offsets_hbm, offsets),
                (fractions_hbm, fractions),
                (group_hbm, group),
                (observed_hbm, observed),
                (sigma_hbm, sigma),
            ]
        )
    ]
    for copy in in_copies:
        copy.start()
    tab_copy = pltpu.make_async_copy(tables, tabs, tab_sem)
    tab_copy.start()
    resp_copies = [
        pltpu.make_async_copy(
            response.at[pl.ds(i * chunk_rows, chunk_rows)],
            resp.at[pl.ds(i * chunk_rows, chunk_rows)],
            resp_sem.at[i],
        )
        for i in range(resp_sem.shape[0])
    ]
    for copy in resp_copies:
        copy.start()

    barrier = pltpu.get_barrier_semaphore()
    for k in range(1, ncx):
        pl.semaphore_signal(
            barrier, inc=1, device_id=(lax.rem(cx + k, ncx), cy), device_id_type=MESH
        )
    for k in range(1, ncy):
        pl.semaphore_signal(
            barrier, inc=1, device_id=(cx, lax.rem(cy + k, ncy)), device_id_type=MESH
        )
    in_copies[0].wait()
    halo_out[0] = latent[:, 0:LANES].astype(BF16)
    halo_out[1] = latent[:, LANES:].astype(BF16)
    pl.semaphore_wait(barrier, ncx + ncy - 2)
    for k in range(1, ncx):
        pl.semaphore_signal(
            ready, inc=1, device_id=(lax.rem(cx + k, ncx), cy), device_id_type=MESH
        )

    def start_halo(at, along):
        copies = []
        for side in range(2):
            step = 1 if side == 0 else -1
            if along == "x":
                to = (lax.rem(cx + step + ncx, ncx), cy)
            else:
                to = (cx, lax.rem(cy + step + ncy, ncy))
            copy = pltpu.make_async_remote_copy(
                src_ref=halo_out.at[at],
                dst_ref=halo_in.at[2 * at + side],
                send_sem=halo_send.at[2 * at + side],
                recv_sem=halo_recv.at[2 * at + side],
                device_id=to,
                device_id_type=MESH,
            )
            copy.start()
            copies.append(copy)
        return copies

    def own_part(x, at):
        both = dot(tabs[2 * at], jnp.concatenate(split(x), axis=1))
        return both[:, :LANES] + both[:, LANES:] + dot(tabs[2 * at + 1], x.astype(BF16))

    def halo_part(copies, at, first):
        place, count = (cx, ncx) if first == 0 else (cy, ncy)
        copies[0].wait_recv()
        copies[1].wait_recv()
        left = halo_in[2 * at]
        right = halo_in[2 * at + 1]
        from_left = dot(tabs[2 * first + 2], left) + dot(tabs[2 * first + 3], left)
        from_right = dot(tabs[2 * first + 4], right) + dot(tabs[2 * first + 5], right)
        zero = jnp.zeros_like(from_left)
        return jnp.where(place > 0, from_left, zero) + jnp.where(
            place < count - 1, from_right, zero
        )

    def along_z(x):
        high, low = split(x)
        return dot(high, tabs[12]) + dot(high, tabs[13]) + dot(low, tabs[12])

    count = ncx * ncy
    me = cx * ncy + cy

    def start_swap(out, into, at):
        def send_to(k, carry):
            to = lax.rem(me + k, count)
            pltpu.make_async_remote_copy(
                src_ref=out.at[to],
                dst_ref=into.at[me],
                send_sem=swap_send.at[at],
                recv_sem=swap_recv.at[at],
                device_id=(to // ncy, lax.rem(to, ncy)),
                device_id_type=MESH,
            ).start()
            return carry

        lax.fori_loop(1, count, send_to, 0, unroll=UNROLL_SENDS)
        into[me] = out[me]

    def all_but_one(ref, sem):
        part = ref.at[pl.ds(0, count - 1)]
        return pltpu.make_async_copy(part, part, sem)

    started = []

    def smooth(x, base, first_work, second_work):
        low, high = x[:, :LANES], x[:, LANES:]
        if base > 0:
            halo_out[base] = low.astype(BF16)
            halo_out[base + 1] = high.astype(BF16)
        low_copies = start_halo(base, "x")
        high_copies = start_halo(base + 1, "y")
        started.extend(low_copies + high_copies)
        first_work()
        low, high = own_part(low, 0), own_part(high, 3)
        low = low + halo_part(low_copies, base, 0)
        halo_out[base + 2] = low.astype(BF16)
        low_copies = start_halo(base + 2, "y")
        high = high + halo_part(high_copies, base + 1, 3)
        halo_out[base + 3] = high.astype(BF16)
        high_copies = start_halo(base + 3, "x")
        started.extend(low_copies + high_copies)
        second_work()
        low, high = own_part(low, 3), own_part(high, 0)
        high = high + halo_part(high_copies, base + 3, 0)
        low = low + halo_part(low_copies, base + 2, 3)
        return along_z(jnp.concatenate([low, high], axis=1))


    def columns_of(row):
        return jnp.broadcast_to(row.astype(F32), (LANES, row.shape[1])).T

    lane_of = lax.broadcasted_iota(jnp.int32, (1, LANES), 1).astype(F32)
    voxels = latent.shape[0]
    depth = latent.shape[1]
    group_rows = 8 * samples
    groups = observed.shape[0]

    def prepare(g, carry):
        rows = pl.ds(pl.multiple_of(g * group_rows, group_rows), group_rows)
        resp_t[g] = resp[rows, :].T
        first = g * 8
        strip = low_index[:, pl.ds(pl.multiple_of(first // LANES * LANES, LANES), LANES)]
        hots = []
        for t in range(8):
            lane = jnp.full((samples, LANES), lax.rem(first, LANES) + t, jnp.int32)
            at = jnp.take_along_axis(strip, lane, axis=1, mode="promise_in_bounds")
            hots.append(one_hot(at, lane_of))
        hot_near[rows, :] = jnp.concatenate(hots, axis=0)
        return carry

    steps = tiles // 8
    per_chunk = steps // len(resp_copies)

    def prepare_chunks(chunks):
        for i in chunks:
            resp_copies[i].wait()
            lax.fori_loop(i * per_chunk, (i + 1) * per_chunk, prepare, 0, unroll=4)

    def index_work():
        for copy in in_copies[1:]:
            copy.wait()
        owner = lax.broadcasted_iota(jnp.int32, (count, 1), 0)
        slot_lane = lax.broadcasted_iota(jnp.int32, (1, slots), 1)
        spread = dot(
            jnp.concatenate([send[...].astype(F32), jnp.zeros((8 - cap, count), F32)], axis=0).astype(BF16),
            one_hot(owner, slot_lane // cap),
        )
        own_lane = lax.broadcasted_iota(jnp.int32, (8, 1), 0) == lax.rem(slot_lane, cap)
        send_row = jnp.sum(jnp.where(own_lane, spread, 0.0), axis=0, keepdims=True)
        send_col = columns_of(send_row)
        for j in range(voxels // LANES):
            hot_out[:, j * LANES : (j + 1) * LANES] = one_hot(send_col, lane_of + j * LANES)
        row_of = lax.broadcasted_iota(jnp.int32, (voxels, 1), 0).astype(F32)
        hot_back[...] = one_hot(row_of, send_row)
        slot_row = lax.broadcasted_iota(jnp.int32, (slots, 1), 0).astype(F32)
        hot_slot[...] = one_hot(slot_row, slot[...].astype(F32))
        below = offsets[...].astype(F32)
        index[...] = jnp.concatenate([below, below + 1.0], axis=0).T.astype(jnp.int32)
        odup[...] = jnp.concatenate([below, below], axis=0).T
        share = fractions[...]
        weight[...] = jnp.concatenate([1.0 - share, share], axis=0).T
        low_index[...] = jnp.where(below >= LANES, below - LANES, below)
        group_of = lax.broadcasted_iota(jnp.int32, (groups, 1), 0).astype(F32)
        hot_group[...] = one_hot(group_of, group[...].astype(F32))
        hot_of_tile[...] = one_hot(columns_of(group[...]), lane_of)
        tab_copy.wait()
        prepare_chunks(CHUNKS_X)

    field = smooth(latent[...], 0, index_work, lambda: prepare_chunks(CHUNKS_Y))
    dens = jnp.exp(field)
    density[...] = dens

    packed = dot(hot_out[...], dens.astype(BF16)).astype(BF16)
    there_out[...] = packed.reshape(there_out.shape)
    pl.semaphore_wait(ready, ncx - 1)
    start_swap(there_out, there_in, 0)
    prepare_chunks(CHUNKS_SWAP)
    slot_col = columns_of(slot[...])
    hot_tile = jnp.concatenate(
        [one_hot(slot_col, lane_of + j * LANES) for j in range(-(-slots // LANES))], axis=1
    )[:, :slots]
    all_but_one(there_in, swap_recv.at[0]).wait()
    block_of[...] = dot(hot_tile, there_in[...].reshape(slots, depth))

    pair_of = lax.broadcasted_iota(jnp.int32, (8, LANES), 0) // 2
    odd_row = lax.rem(lax.broadcasted_iota(jnp.int32, (8, LANES), 0), 2)
    upper = lax.broadcasted_iota(jnp.int32, (8, LANES), 1) // samples
    keep = [(pair_of == j) & (odd_row == upper) for j in range(4)]
    masks = [jnp.where(k, 1.0, 0.0) for k in keep]
    high_lane = lax.broadcasted_iota(jnp.int32, (1, LANES), 1) >= samples
    masks = [m.astype(BF16) for m in masks]
    set_of = 8 * SET

    def forward(i, carry):
        first = pl.multiple_of(i * set_of, set_of)
        rows = pl.ds(first, set_of)
        at = index[rows, :]
        near = at & (LANES - 1)
        low = jnp.take_along_axis(
            block_of[rows, 0:LANES], near, axis=1, mode="promise_in_bounds"
        )
        far = jnp.take_along_axis(
            block_of[rows, LANES : 2 * LANES], near, axis=1, mode="promise_in_bounds"
        )
        terms = jnp.where(at < LANES, low, far) * weight[rows, :]
        sample = (terms + pltpu.roll(terms, samples, 1)).astype(BF16)
        lefts = []
        for j in range(SET):
            own = sample[8 * j : 8 * j + 8]
            lefts.append(jnp.concatenate([own * m for m in masks], axis=1))
        preds = []
        for j in range(SET):
            at_row = pl.multiple_of(first * samples + j * group_rows, group_rows)
            preds.append(dot(lefts[j], resp[pl.ds(at_row, group_rows), :]))
        tile_pred[rows, :] = jnp.concatenate(preds, axis=0)
        return carry

    lax.fori_loop(0, tiles // set_of, forward, 0)

    high, low = split(tile_pred[...])
    total = dot(hot_group[...], high) + dot(hot_group[...], low)
    predicted[...] = total
    resid = (total - observed[...]) / (sigma[...] * sigma[...])
    resid = jnp.concatenate([resid, jnp.zeros((LANES - groups, LANES), F32)], axis=0)
    tile_resid[...] = dot(hot_of_tile[...], resid.astype(BF16))

    masks2 = [jnp.concatenate([m, m], axis=0) for m in masks]

    def backward(i, carry):
        first = pl.multiple_of(i * set_of, set_of)
        rows = pl.ds(first, set_of)
        tr = tile_resid[rows, :].astype(BF16)
        backs = [dot(tr[8 * j : 8 * j + 8], resp_t[i * SET + j]) for j in range(SET)]
        own = jnp.concatenate(
            [
                sum(
                    jnp.where(keep[n], back[:, n * LANES : (n + 1) * LANES], 0.0)
                    for n in range(4)
                )
                for back in backs
            ],
            axis=0,
        )
        own = own + pltpu.roll(own, samples, 1)
        parts = own * weight[rows, :]
        turned = pltpu.roll(parts, samples, 1)
        v_low = jnp.where(high_lane, turned, parts)
        v_high = jnp.where(high_lane, parts, turned)
        is_far = odup[rows, :] >= LANES
        kinds = [
            jnp.where(is_far, 0.0, v_low),
            jnp.where(is_far, 0.0, v_high),
            jnp.where(is_far, v_low, 0.0),
            jnp.where(is_far, v_high, 0.0),
        ]
        lefts = []
        for j in range(SET):
            own_kinds = [kind[8 * j : 8 * j + 8] for kind in kinds]
            near = jnp.concatenate(own_kinds[0:2], axis=0).astype(BF16)
            far = jnp.concatenate(own_kinds[2:4], axis=0).astype(BF16)
            lefts.append(
                jnp.concatenate(
                    [
                        jnp.concatenate([near * m for m in masks2], axis=1),
                        jnp.concatenate([far * m for m in masks2], axis=1),
                    ],
                    axis=0,
                )
            )
        outs = []
        for j in range(SET):
            at_row = pl.multiple_of(first * samples + j * group_rows, group_rows)
            outs.append(dot(lefts[j], hot_near[pl.ds(at_row, group_rows), :]))
        lower_near = jnp.concatenate([out[0:8] for out in outs], axis=0)
        raised_near = jnp.concatenate([out[8:16] for out in outs], axis=0)
        lower_far = jnp.concatenate([out[16:24] for out in outs], axis=0)
        raised_far = jnp.concatenate([out[24:32] for out in outs], axis=0)
        raised = jnp.concatenate([raised_near, raised_far], axis=1)
        lower = jnp.concatenate([lower_near, lower_far], axis=1)
        tile_grad[rows, :] = lower + pltpu.roll(raised, 1, 1)
        return carry

    lax.fori_loop(0, tiles // set_of, backward, 0)

    high, low = split(tile_grad[...])
    slot_grad = dot(hot_slot[...], high) + dot(hot_slot[...], low)

    back_out[...] = slot_grad.astype(BF16).reshape(back_out.shape)
    start_swap(back_out, back_in, 1)
    all_but_one(back_in, swap_recv.at[1]).wait()
    dens_grad = dot(hot_back[...], back_in[...].reshape(slots, depth))

    field = density[...] * dens_grad
    field = smooth(field, 4, lambda: None, lambda: None)
    gradient[...] = latent[...] + field
    for copy in started:
        copy.wait_send()
    all_but_one(there_out, swap_send.at[0]).wait()
    all_but_one(back_out, swap_send.at[1]).wait()


def hand_out(field, stars, field_out, stars_out):
    field_out[...] = field[...]
    stars_out[...] = stars[...]


def on_device(
    latent, observed, sigma, response, offsets, fractions, tile_group, tile_slot, send_index
):
    ncx, ncy = lax.axis_size("cx"), lax.axis_size("cy")
    rows_x, rows_y, depth = latent.shape
    tiles, samples, star_tile = response.shape
    groups = observed.shape[0] // star_tile
    cap = send_index.shape[2]
    voxels = rows_x * rows_y
    slots = ncx * ncy * cap
    tables = smoothing_tables(rows_x, rows_y, depth)
    chunks = 8
    vmem = pl.BlockSpec(memory_space=pltpu.VMEM)
    anywhere = pl.BlockSpec(memory_space=pltpu.HBM)
    gradient, predicted = pl.pallas_call(
        functools.partial(kernel, ncx, ncy, cap),
        out_shape=(
            jax.ShapeDtypeStruct((voxels, depth), F32),
            jax.ShapeDtypeStruct((groups, star_tile), F32),
        ),
        in_specs=[anywhere] * 10,
        out_specs=(vmem, vmem),
        scratch_shapes=[
            pltpu.VMEM((voxels, depth), F32),
            pltpu.VMEM((groups, star_tile), F32),
            pltpu.VMEM((groups, star_tile), F32),
            pltpu.VMEM((samples, tiles), jnp.int32),
            pltpu.VMEM((samples, tiles), F32),
            pltpu.VMEM((1, tiles), jnp.int32),
            pltpu.VMEM((1, tiles), jnp.int32),
            pltpu.VMEM((cap, ncx * ncy), jnp.int32),
            pltpu.VMEM((tiles * samples, star_tile), BF16),
            pltpu.VMEM((tiles // 8, star_tile, 8 * samples), BF16),
            pltpu.VMEM((tiles * samples, LANES), BF16),
            pltpu.VMEM(tables.shape, BF16),
            pltpu.VMEM((8, voxels, depth // 2), BF16),
            pltpu.VMEM((16, voxels, depth // 2), BF16),
            pltpu.VMEM((ncx * ncy, cap, depth), BF16),
            pltpu.VMEM((ncx * ncy, cap, depth), BF16),
            pltpu.VMEM((ncx * ncy, cap, depth), BF16),
            pltpu.VMEM((ncx * ncy, cap, depth), BF16),
            pltpu.VMEM((tiles, 2 * samples), jnp.int32),
            pltpu.VMEM((tiles, 2 * samples), F32),
            pltpu.VMEM((tiles, 2 * samples), F32),
            pltpu.VMEM((samples, tiles), F32),
            pltpu.VMEM((tiles, depth), F32),
            pltpu.VMEM((tiles, star_tile), F32),
            pltpu.VMEM((tiles, star_tile), F32),
            pltpu.VMEM((tiles, depth), F32),
            pltpu.VMEM((slots, voxels), BF16),
            pltpu.VMEM((voxels, slots), BF16),
            pltpu.VMEM((slots, tiles), BF16),
            pltpu.VMEM((groups, tiles), BF16),
            pltpu.VMEM((tiles, LANES), BF16),
            pltpu.VMEM((voxels, depth), F32),
            pltpu.SemaphoreType.DMA((8,)),
            pltpu.SemaphoreType.DMA((chunks,)),
            pltpu.SemaphoreType.DMA,
            pltpu.SemaphoreType.DMA((16,)),
            pltpu.SemaphoreType.DMA((16,)),
            pltpu.SemaphoreType.DMA((2,)),
            pltpu.SemaphoreType.DMA((2,)),
            pltpu.SemaphoreType.REGULAR,
        ],
        compiler_params=pltpu.CompilerParams(
            collective_id=0, has_side_effects=True, vmem_limit_bytes=62 * 1024 * 1024
        ),
        name="dust_map",
    )(
        latent.reshape(voxels, depth),
        observed.reshape(groups, star_tile),
        sigma.reshape(groups, star_tile),
        response.reshape(tiles * samples, star_tile),
        offsets,
        fractions,
        tile_group.reshape(1, tiles),
        tile_slot.reshape(1, tiles),
        send_index.transpose(0, 2, 1).reshape(cap, ncx * ncy),
        jnp.asarray(tables),
    )
    gradient, predicted = pl.pallas_call(
        hand_out,
        out_shape=(
            jax.ShapeDtypeStruct((voxels, depth), F32),
            jax.ShapeDtypeStruct((groups, star_tile), F32),
        ),
        in_specs=[vmem] * 2,
        out_specs=(vmem, vmem),
        name="hand_out",
    )(gradient, predicted)
    return gradient.reshape(latent.shape), predicted.reshape(-1)


def solution(mesh):
    placed = (
        P("cx", "cy", None),
        P(("cx", "cy")),
        P(("cx", "cy")),
        P(("cx", "cy"), None, None),
        P(None, ("cx", "cy")),
        P(None, ("cx", "cy")),
        P(("cx", "cy")),
        P(("cx", "cy")),
        P(("cx", "cy"), None, None),
    )
    return jax.shard_map(
        on_device,
        mesh=mesh,
        in_specs=placed,
        out_specs=(P("cx", "cy", None), P(("cx", "cy"))),
        check_vma=False,
    )
```

```python
import functools
import itertools

import jax
import jax.numpy as jnp
import ml_dtypes
import numpy as np
from jax import lax
from jax.experimental import pallas as pl
from jax.experimental.pallas import tpu as pltpu
from jax.sharding import PartitionSpec as P

F32, BF16 = jnp.float32, jnp.bfloat16
MESH = pl.DeviceIdType.MESH
LANES = 128
SET = 32
CHUNKS_X, CHUNKS_Y, CHUNKS_SWAP = (0, 1), (2, 3, 4), (5, 6, 7)


def smoothing_tables(rows_x, rows_y, depth):
    shifts = np.arange(-16, 17).astype(np.float32)
    scaled = np.sqrt(np.float32(3.0)) * np.abs(shifts) / np.float32(8.0)
    raw = (np.float32(1.0) + scaled) * np.exp(-scaled)
    taps = np.float32(0.8) * raw / np.sqrt(np.sum(raw * raw))

    def band(length, start):
        shift = np.arange(length)[None, :] + start - np.arange(length)[:, None]
        inside = np.abs(shift) <= 16
        return np.where(inside, taps[np.clip(shift + 16, 0, 32)], 0).astype(np.float32)

    whole = [np.kron(band(rows_x, s), np.eye(rows_y)) for s in (0, -rows_x, rows_x)]
    whole += [np.kron(np.eye(rows_x), band(rows_y, s)) for s in (0, -rows_y, rows_y)]
    whole += [band(depth, 0)]
    parts = []
    for table in whole:
        table = table.astype(np.float32)
        high = table.astype(ml_dtypes.bfloat16)
        parts += [high, (table - high.astype(np.float32)).astype(ml_dtypes.bfloat16)]
    return np.stack(parts)


def dot(a, b):
    return lax.dot_general(a, b, (((1,), (0,)), ((), ())), preferred_element_type=F32)


def dot_t(a, b):
    return lax.dot_general(a, b, (((1,), (1,)), ((), ())), preferred_element_type=F32)


def split(x):
    high = x.astype(BF16)
    return high, (x - high.astype(F32)).astype(BF16)


def one_hot(a, b):
    return jnp.where(a == b, 1.0, 0.0).astype(BF16)


def far_first(ring_z, ring_y, ring_x):
    def links(step):
        dz, dc, dy, dx = step
        return (
            min(dz, ring_z - dz) + min(dy, ring_y - dy) + min(dx, ring_x - dx) + 0.5 * dc
        )

    steps = itertools.product(range(ring_z), range(2), range(ring_y), range(ring_x))
    return sorted((step for step in steps if any(step)), key=links, reverse=True)


def kernel(
    ncx, ncy, cap,
    latent_hbm, observed_hbm, sigma_hbm, response, offsets_hbm, fractions_hbm, group_hbm,
    slot_hbm, send_hbm, tables,
    gradient, predicted,
    latent, observed, sigma, offsets, fractions, group, slot, send, resp, resp_t, hot_near, tabs,
    halo_out, halo_in, there_out, there_in, back_out, back_in,
    index, weight, odup, low_index, block_of, tile_pred, tile_resid, tile_grad,
    hot_out, hot_back, hot_slot, hot_group, hot_of_tile, density,
    in_sem, resp_sem, tab_sem, halo_send, halo_recv, swap_send, swap_recv, ready,
):
    cx, cy = lax.axis_index("cx"), lax.axis_index("cy")
    tiles = slot.shape[1]
    slots = ncx * ncy * cap
    samples = offsets.shape[0]
    chunk_rows = resp.shape[0] // resp_sem.shape[0]

    in_copies = [
        pltpu.make_async_copy(source, target, in_sem.at[i])
        for i, (source, target) in enumerate(
            [
                (latent_hbm, latent),
                (send_hbm, send),
                (slot_hbm, slot),
                (offsets_hbm, offsets),
                (fractions_hbm, fractions),
                (group_hbm, group),
                (observed_hbm, observed),
                (sigma_hbm, sigma),
            ]
        )
    ]
    for copy in in_copies:
        copy.start()
    tab_copy = pltpu.make_async_copy(tables, tabs, tab_sem)
    tab_copy.start()
    resp_copies = [
        pltpu.make_async_copy(
            response.at[pl.ds(i * chunk_rows, chunk_rows)],
            resp.at[pl.ds(i * chunk_rows, chunk_rows)],
            resp_sem.at[i],
        )
        for i in range(resp_sem.shape[0])
    ]
    for copy in resp_copies:
        copy.start()

    barrier = pltpu.get_barrier_semaphore()
    for k in range(1, ncx):
        pl.semaphore_signal(
            barrier, inc=1, device_id=(lax.rem(cx + k, ncx), cy), device_id_type=MESH
        )
    for k in range(1, ncy):
        pl.semaphore_signal(
            barrier, inc=1, device_id=(cx, lax.rem(cy + k, ncy)), device_id_type=MESH
        )
    in_copies[0].wait()
    halo_out[0] = latent[:, 0:LANES].astype(BF16)
    halo_out[1] = latent[:, LANES:].astype(BF16)
    pl.semaphore_wait(barrier, ncx + ncy - 2)
    for k in range(1, ncx):
        pl.semaphore_signal(
            ready, inc=1, device_id=(lax.rem(cx + k, ncx), cy), device_id_type=MESH
        )

    def start_halo(at, along):
        copies = []
        for side in range(2):
            step = 1 if side == 0 else -1
            if along == "x":
                to = (lax.rem(cx + step + ncx, ncx), cy)
            else:
                to = (cx, lax.rem(cy + step + ncy, ncy))
            copy = pltpu.make_async_remote_copy(
                src_ref=halo_out.at[at],
                dst_ref=halo_in.at[2 * at + side],
                send_sem=halo_send.at[2 * at + side],
                recv_sem=halo_recv.at[2 * at + side],
                device_id=to,
                device_id_type=MESH,
            )
            copy.start()
            copies.append(copy)
        return copies

    def own_part(x, at):
        both = dot(tabs[2 * at], jnp.concatenate(split(x), axis=1))
        return both[:, :LANES] + both[:, LANES:] + dot(tabs[2 * at + 1], x.astype(BF16))

    def halo_part(copies, at, first):
        place, count = (cx, ncx) if first == 0 else (cy, ncy)
        copies[0].wait_recv()
        copies[1].wait_recv()
        left = halo_in[2 * at]
        right = halo_in[2 * at + 1]
        from_left = dot(tabs[2 * first + 2], left) + dot(tabs[2 * first + 3], left)
        from_right = dot(tabs[2 * first + 4], right) + dot(tabs[2 * first + 5], right)
        zero = jnp.zeros_like(from_left)
        return jnp.where(place > 0, from_left, zero) + jnp.where(
            place < count - 1, from_right, zero
        )

    def along_z(x):
        high, low = split(x)
        return dot(high, tabs[12]) + dot(high, tabs[13]) + dot(low, tabs[12])

    count = ncx * ncy
    me = cx * ncy + cy
    ring_x = 4 if ncy % 4 == 0 else ncy
    ring_y, ring_z = ncy // ring_x, ncx // 2
    at_z, at_core = cx // 2, lax.rem(cx, 2)
    at_y, at_x = cy // ring_x, lax.rem(cy, ring_x)

    def start_swap(out, into, at):
        for dz, dc, dy, dx in far_first(ring_z, ring_y, ring_x):
            to_cx = lax.rem(at_z + dz, ring_z) * 2 + lax.rem(at_core + dc, 2)
            to_cy = lax.rem(at_y + dy, ring_y) * ring_x + lax.rem(at_x + dx, ring_x)
            pltpu.make_async_remote_copy(
                src_ref=out.at[to_cx * ncy + to_cy],
                dst_ref=into.at[me],
                send_sem=swap_send.at[at],
                recv_sem=swap_recv.at[at],
                device_id=(to_cx, to_cy),
                device_id_type=MESH,
            ).start()
        into[me] = out[me]

    def all_but_one(ref, sem):
        part = ref.at[pl.ds(0, count - 1)]
        return pltpu.make_async_copy(part, part, sem)

    started = []

    def smooth(x, base, first_work, second_work):
        low, high = x[:, :LANES], x[:, LANES:]
        if base > 0:
            halo_out[base] = low.astype(BF16)
            halo_out[base + 1] = high.astype(BF16)
        low_copies = start_halo(base, "x")
        high_copies = start_halo(base + 1, "y")
        started.extend(low_copies + high_copies)
        first_work()
        low, high = own_part(low, 0), own_part(high, 3)
        low = low + halo_part(low_copies, base, 0)
        halo_out[base + 2] = low.astype(BF16)
        low_copies = start_halo(base + 2, "y")
        high = high + halo_part(high_copies, base + 1, 3)
        halo_out[base + 3] = high.astype(BF16)
        high_copies = start_halo(base + 3, "x")
        started.extend(low_copies + high_copies)
        second_work()
        low, high = own_part(low, 3), own_part(high, 0)
        high = high + halo_part(high_copies, base + 3, 0)
        low = low + halo_part(low_copies, base + 2, 3)
        return along_z(jnp.concatenate([low, high], axis=1))


    def columns_of(row):
        return jnp.broadcast_to(row.astype(F32), (LANES, row.shape[1])).T

    lane_of = lax.broadcasted_iota(jnp.int32, (1, LANES), 1).astype(F32)
    voxels = latent.shape[0]
    depth = latent.shape[1]
    group_rows = 8 * samples
    groups = observed.shape[0]

    def prepare(g, carry):
        rows = pl.ds(pl.multiple_of(g * group_rows, group_rows), group_rows)
        resp_t[g] = resp[rows, :].T
        first = g * 8
        strip = low_index[:, pl.ds(pl.multiple_of(first // LANES * LANES, LANES), LANES)]
        hots = []
        for t in range(8):
            lane = jnp.full((samples, LANES), lax.rem(first, LANES) + t, jnp.int32)
            at = jnp.take_along_axis(strip, lane, axis=1, mode="promise_in_bounds")
            hots.append(one_hot(at, lane_of))
        hot_near[rows, :] = jnp.concatenate(hots, axis=0)
        return carry

    steps = tiles // 8
    per_chunk = steps // len(resp_copies)

    def prepare_chunks(chunks):
        for i in chunks:
            resp_copies[i].wait()
            lax.fori_loop(i * per_chunk, (i + 1) * per_chunk, prepare, 0, unroll=4)

    def index_work():
        for copy in in_copies[1:]:
            copy.wait()
        owner = lax.broadcasted_iota(jnp.int32, (count, 1), 0)
        slot_lane = lax.broadcasted_iota(jnp.int32, (1, slots), 1)
        spread = dot(
            jnp.concatenate([send[...].astype(F32), jnp.zeros((8 - cap, count), F32)], axis=0).astype(BF16),
            one_hot(owner, slot_lane // cap),
        )
        own_lane = lax.broadcasted_iota(jnp.int32, (8, 1), 0) == lax.rem(slot_lane, cap)
        send_row = jnp.sum(jnp.where(own_lane, spread, 0.0), axis=0, keepdims=True)
        send_col = columns_of(send_row)
        for j in range(voxels // LANES):
            hot_out[:, j * LANES : (j + 1) * LANES] = one_hot(send_col, lane_of + j * LANES)
        row_of = lax.broadcasted_iota(jnp.int32, (voxels, 1), 0).astype(F32)
        hot_back[...] = one_hot(row_of, send_row)
        slot_row = lax.broadcasted_iota(jnp.int32, (slots, 1), 0).astype(F32)
        hot_slot[...] = one_hot(slot_row, slot[...].astype(F32))
        below = offsets[...].astype(F32)
        index[...] = jnp.concatenate([below, below + 1.0], axis=0).T.astype(jnp.int32)
        odup[...] = jnp.concatenate([below, below], axis=0).T
        share = fractions[...]
        weight[...] = jnp.concatenate([1.0 - share, share], axis=0).T
        low_index[...] = jnp.where(below >= LANES, below - LANES, below)
        group_of = lax.broadcasted_iota(jnp.int32, (groups, 1), 0).astype(F32)
        hot_group[...] = one_hot(group_of, group[...].astype(F32))
        hot_of_tile[...] = one_hot(columns_of(group[...]), lane_of)
        tab_copy.wait()
        prepare_chunks(CHUNKS_X)

    field = smooth(latent[...], 0, index_work, lambda: prepare_chunks(CHUNKS_Y))
    dens = jnp.exp(field)
    density[...] = dens

    packed = dot(hot_out[...], dens.astype(BF16)).astype(BF16)
    there_out[...] = packed.reshape(there_out.shape)
    pl.semaphore_wait(ready, ncx - 1)
    start_swap(there_out, there_in, 0)
    prepare_chunks(CHUNKS_SWAP)
    slot_col = columns_of(slot[...])
    hot_tile = jnp.concatenate(
        [one_hot(slot_col, lane_of + j * LANES) for j in range(-(-slots // LANES))], axis=1
    )[:, :slots]
    all_but_one(there_in, swap_recv.at[0]).wait()
    block_of[...] = dot(hot_tile, there_in[...].reshape(slots, depth))

    pair_of = lax.broadcasted_iota(jnp.int32, (8, LANES), 0) // 2
    odd_row = lax.rem(lax.broadcasted_iota(jnp.int32, (8, LANES), 0), 2)
    upper = lax.broadcasted_iota(jnp.int32, (8, LANES), 1) // samples
    keep = [(pair_of == j) & (odd_row == upper) for j in range(4)]
    masks = [jnp.where(k, 1.0, 0.0) for k in keep]
    high_lane = lax.broadcasted_iota(jnp.int32, (1, LANES), 1) >= samples
    masks = [m.astype(BF16) for m in masks]
    set_of = 8 * SET

    def forward(i, carry):
        first = pl.multiple_of(i * set_of, set_of)
        rows = pl.ds(first, set_of)
        at = index[rows, :]
        near = at & (LANES - 1)
        low = jnp.take_along_axis(
            block_of[rows, 0:LANES], near, axis=1, mode="promise_in_bounds"
        )
        far = jnp.take_along_axis(
            block_of[rows, LANES : 2 * LANES], near, axis=1, mode="promise_in_bounds"
        )
        terms = jnp.where(at < LANES, low, far) * weight[rows, :]
        sample = (terms + pltpu.roll(terms, samples, 1)).astype(BF16)
        lefts = []
        for j in range(SET):
            own = sample[8 * j : 8 * j + 8]
            lefts.append(jnp.concatenate([own * m for m in masks], axis=1))
        preds = []
        for j in range(SET):
            at_row = pl.multiple_of(first * samples + j * group_rows, group_rows)
            preds.append(dot(lefts[j], resp[pl.ds(at_row, group_rows), :]))
        tile_pred[rows, :] = jnp.concatenate(preds, axis=0)
        return carry

    lax.fori_loop(0, tiles // set_of, forward, 0)

    high, low = split(tile_pred[...])
    total = dot(hot_group[...], high) + dot(hot_group[...], low)
    predicted[...] = total
    resid = (total - observed[...]) / (sigma[...] * sigma[...])
    resid = jnp.concatenate([resid, jnp.zeros((LANES - groups, LANES), F32)], axis=0)
    tile_resid[...] = dot(hot_of_tile[...], resid.astype(BF16))

    masks2 = [jnp.concatenate([m, m], axis=0) for m in masks]

    def backward(i, carry):
        first = pl.multiple_of(i * set_of, set_of)
        rows = pl.ds(first, set_of)
        tr = tile_resid[rows, :].astype(BF16)
        backs = [dot(tr[8 * j : 8 * j + 8], resp_t[i * SET + j]) for j in range(SET)]
        own = jnp.concatenate(
            [
                sum(
                    jnp.where(keep[n], back[:, n * LANES : (n + 1) * LANES], 0.0)
                    for n in range(4)
                )
                for back in backs
            ],
            axis=0,
        )
        own = own + pltpu.roll(own, samples, 1)
        parts = own * weight[rows, :]
        turned = pltpu.roll(parts, samples, 1)
        v_low = jnp.where(high_lane, turned, parts)
        v_high = jnp.where(high_lane, parts, turned)
        is_far = odup[rows, :] >= LANES
        kinds = [
            jnp.where(is_far, 0.0, v_low),
            jnp.where(is_far, 0.0, v_high),
            jnp.where(is_far, v_low, 0.0),
            jnp.where(is_far, v_high, 0.0),
        ]
        lefts = []
        for j in range(SET):
            own_kinds = [kind[8 * j : 8 * j + 8] for kind in kinds]
            near = jnp.concatenate(own_kinds[0:2], axis=0).astype(BF16)
            far = jnp.concatenate(own_kinds[2:4], axis=0).astype(BF16)
            lefts.append(
                jnp.concatenate(
                    [
                        jnp.concatenate([near * m for m in masks2], axis=1),
                        jnp.concatenate([far * m for m in masks2], axis=1),
                    ],
                    axis=0,
                )
            )
        outs = []
        for j in range(SET):
            at_row = pl.multiple_of(first * samples + j * group_rows, group_rows)
            outs.append(dot(lefts[j], hot_near[pl.ds(at_row, group_rows), :]))
        lower_near = jnp.concatenate([out[0:8] for out in outs], axis=0)
        raised_near = jnp.concatenate([out[8:16] for out in outs], axis=0)
        lower_far = jnp.concatenate([out[16:24] for out in outs], axis=0)
        raised_far = jnp.concatenate([out[24:32] for out in outs], axis=0)
        raised = jnp.concatenate([raised_near, raised_far], axis=1)
        lower = jnp.concatenate([lower_near, lower_far], axis=1)
        tile_grad[rows, :] = lower + pltpu.roll(raised, 1, 1)
        return carry

    lax.fori_loop(0, tiles // set_of, backward, 0)

    high, low = split(tile_grad[...])
    slot_grad = dot(hot_slot[...], high) + dot(hot_slot[...], low)

    back_out[...] = slot_grad.astype(BF16).reshape(back_out.shape)
    start_swap(back_out, back_in, 1)
    all_but_one(back_in, swap_recv.at[1]).wait()
    dens_grad = dot(hot_back[...], back_in[...].reshape(slots, depth))

    field = density[...] * dens_grad
    field = smooth(field, 4, lambda: None, lambda: None)
    gradient[...] = latent[...] + field
    for copy in started:
        copy.wait_send()
    all_but_one(there_out, swap_send.at[0]).wait()
    all_but_one(back_out, swap_send.at[1]).wait()


def hand_out(field, stars, field_out, stars_out):
    field_out[...] = field[...]
    stars_out[...] = stars[...]


def on_device(
    latent, observed, sigma, response, offsets, fractions, tile_group, tile_slot, send_index
):
    ncx, ncy = lax.axis_size("cx"), lax.axis_size("cy")
    rows_x, rows_y, depth = latent.shape
    tiles, samples, star_tile = response.shape
    groups = observed.shape[0] // star_tile
    cap = send_index.shape[2]
    voxels = rows_x * rows_y
    slots = ncx * ncy * cap
    tables = smoothing_tables(rows_x, rows_y, depth)
    chunks = 8
    vmem = pl.BlockSpec(memory_space=pltpu.VMEM)
    anywhere = pl.BlockSpec(memory_space=pltpu.HBM)
    gradient, predicted = pl.pallas_call(
        functools.partial(kernel, ncx, ncy, cap),
        out_shape=(
            jax.ShapeDtypeStruct((voxels, depth), F32),
            jax.ShapeDtypeStruct((groups, star_tile), F32),
        ),
        in_specs=[anywhere] * 10,
        out_specs=(vmem, vmem),
        scratch_shapes=[
            pltpu.VMEM((voxels, depth), F32),
            pltpu.VMEM((groups, star_tile), F32),
            pltpu.VMEM((groups, star_tile), F32),
            pltpu.VMEM((samples, tiles), jnp.int32),
            pltpu.VMEM((samples, tiles), F32),
            pltpu.VMEM((1, tiles), jnp.int32),
            pltpu.VMEM((1, tiles), jnp.int32),
            pltpu.VMEM((cap, ncx * ncy), jnp.int32),
            pltpu.VMEM((tiles * samples, star_tile), BF16),
            pltpu.VMEM((tiles // 8, star_tile, 8 * samples), BF16),
            pltpu.VMEM((tiles * samples, LANES), BF16),
            pltpu.VMEM(tables.shape, BF16),
            pltpu.VMEM((8, voxels, depth // 2), BF16),
            pltpu.VMEM((16, voxels, depth // 2), BF16),
            pltpu.VMEM((ncx * ncy, cap, depth), BF16),
            pltpu.VMEM((ncx * ncy, cap, depth), BF16),
            pltpu.VMEM((ncx * ncy, cap, depth), BF16),
            pltpu.VMEM((ncx * ncy, cap, depth), BF16),
            pltpu.VMEM((tiles, 2 * samples), jnp.int32),
            pltpu.VMEM((tiles, 2 * samples), F32),
            pltpu.VMEM((tiles, 2 * samples), F32),
            pltpu.VMEM((samples, tiles), F32),
            pltpu.VMEM((tiles, depth), F32),
            pltpu.VMEM((tiles, star_tile), F32),
            pltpu.VMEM((tiles, star_tile), F32),
            pltpu.VMEM((tiles, depth), F32),
            pltpu.VMEM((slots, voxels), BF16),
            pltpu.VMEM((voxels, slots), BF16),
            pltpu.VMEM((slots, tiles), BF16),
            pltpu.VMEM((groups, tiles), BF16),
            pltpu.VMEM((tiles, LANES), BF16),
            pltpu.VMEM((voxels, depth), F32),
            pltpu.SemaphoreType.DMA((8,)),
            pltpu.SemaphoreType.DMA((chunks,)),
            pltpu.SemaphoreType.DMA,
            pltpu.SemaphoreType.DMA((16,)),
            pltpu.SemaphoreType.DMA((16,)),
            pltpu.SemaphoreType.DMA((2,)),
            pltpu.SemaphoreType.DMA((2,)),
            pltpu.SemaphoreType.REGULAR,
        ],
        compiler_params=pltpu.CompilerParams(
            collective_id=0, has_side_effects=True, vmem_limit_bytes=62 * 1024 * 1024
        ),
        name="dust_map",
    )(
        latent.reshape(voxels, depth),
        observed.reshape(groups, star_tile),
        sigma.reshape(groups, star_tile),
        response.reshape(tiles * samples, star_tile),
        offsets,
        fractions,
        tile_group.reshape(1, tiles),
        tile_slot.reshape(1, tiles),
        send_index.transpose(0, 2, 1).reshape(cap, ncx * ncy),
        jnp.asarray(tables),
    )
    gradient, predicted = pl.pallas_call(
        hand_out,
        out_shape=(
            jax.ShapeDtypeStruct((voxels, depth), F32),
            jax.ShapeDtypeStruct((groups, star_tile), F32),
        ),
        in_specs=[vmem] * 2,
        out_specs=(vmem, vmem),
        name="hand_out",
    )(gradient, predicted)
    return gradient.reshape(latent.shape), predicted.reshape(-1)


def solution(mesh):
    placed = (
        P("cx", "cy", None),
        P(("cx", "cy")),
        P(("cx", "cy")),
        P(("cx", "cy"), None, None),
        P(None, ("cx", "cy")),
        P(None, ("cx", "cy")),
        P(("cx", "cy")),
        P(("cx", "cy")),
        P(("cx", "cy"), None, None),
    )
    return jax.shard_map(
        on_device,
        mesh=mesh,
        in_specs=placed,
        out_specs=(P("cx", "cy", None), P(("cx", "cy"))),
        check_vma=False,
    )
```

```python
import functools
import itertools

import jax
import jax.numpy as jnp
import ml_dtypes
import numpy as np
from jax import lax
from jax.experimental import pallas as pl
from jax.experimental.pallas import tpu as pltpu
from jax.sharding import PartitionSpec as P

F32, BF16 = jnp.float32, jnp.bfloat16
MESH = pl.DeviceIdType.MESH
LANES = 128
SET = 64
CHUNKS_X, CHUNKS_Y, CHUNKS_SWAP = tuple(range(2)), tuple(range(2, 6)), tuple(range(6, 16))


def smoothing_tables(rows_x, rows_y, depth):
    shifts = np.arange(-16, 17).astype(np.float32)
    scaled = np.sqrt(np.float32(3.0)) * np.abs(shifts) / np.float32(8.0)
    raw = (np.float32(1.0) + scaled) * np.exp(-scaled)
    taps = np.float32(0.8) * raw / np.sqrt(np.sum(raw * raw))

    def band(length, start):
        shift = np.arange(length)[None, :] + start - np.arange(length)[:, None]
        inside = np.abs(shift) <= 16
        return np.where(inside, taps[np.clip(shift + 16, 0, 32)], 0).astype(np.float32)

    whole = [np.kron(band(rows_x, s), np.eye(rows_y)) for s in (0, -rows_x, rows_x)]
    whole += [np.kron(np.eye(rows_x), band(rows_y, s)) for s in (0, -rows_y, rows_y)]
    whole += [band(depth, 0)]
    parts = []
    for table in whole:
        table = table.astype(np.float32)
        high = table.astype(ml_dtypes.bfloat16)
        parts += [high, (table - high.astype(np.float32)).astype(ml_dtypes.bfloat16)]
    return np.stack(parts)


def dot(a, b):
    return lax.dot_general(a, b, (((1,), (0,)), ((), ())), preferred_element_type=F32)


def dot_t(a, b):
    return lax.dot_general(a, b, (((1,), (1,)), ((), ())), preferred_element_type=F32)


def split(x):
    high = x.astype(BF16)
    return high, (x - high.astype(F32)).astype(BF16)


def one_hot(a, b):
    return jnp.where(a == b, 1.0, 0.0).astype(BF16)


def far_first(ring_z, ring_y, ring_x):
    def links(step):
        dz, dc, dy, dx = step
        return (
            min(dz, ring_z - dz) + min(dy, ring_y - dy) + min(dx, ring_x - dx) + 0.5 * dc
        )

    steps = itertools.product(range(ring_z), range(2), range(ring_y), range(ring_x))
    return sorted((step for step in steps if any(step)), key=links, reverse=True)


def kernel(
    ncx, ncy, cap,
    latent_hbm, observed_hbm, sigma_hbm, response, offsets_hbm, fractions_hbm, group_hbm,
    slot_hbm, send_hbm, tables,
    gradient, predicted,
    latent, observed, sigma, offsets, fractions, group, slot, send, resp, resp_t, hot_near, tabs,
    halo_out, halo_in, there_out, there_in, back_out, back_in,
    index, weight, odup, low_index, block_of, tile_pred, tile_resid, tile_grad,
    hot_out, hot_back, hot_slot, hot_group, hot_of_tile, density,
    in_sem, resp_sem, tab_sem, halo_send, halo_recv, swap_send, swap_recv, ready,
):
    cx, cy = lax.axis_index("cx"), lax.axis_index("cy")
    tiles = slot.shape[1]
    slots = ncx * ncy * cap
    samples = offsets.shape[0]
    chunk_rows = resp.shape[0] // resp_sem.shape[0]

    in_copies = [
        pltpu.make_async_copy(source, target, in_sem.at[i])
        for i, (source, target) in enumerate(
            [
                (latent_hbm, latent),
                (send_hbm, send),
                (slot_hbm, slot),
                (offsets_hbm, offsets),
                (fractions_hbm, fractions),
                (group_hbm, group),
                (observed_hbm, observed),
                (sigma_hbm, sigma),
            ]
        )
    ]
    for copy in in_copies:
        copy.start()
    tab_copy = pltpu.make_async_copy(tables, tabs, tab_sem)
    tab_copy.start()
    resp_copies = [
        pltpu.make_async_copy(
            response.at[pl.ds(i * chunk_rows, chunk_rows)],
            resp.at[pl.ds(i * chunk_rows, chunk_rows)],
            resp_sem.at[i],
        )
        for i in range(resp_sem.shape[0])
    ]
    for copy in resp_copies:
        copy.start()

    barrier = pltpu.get_barrier_semaphore()
    for k in range(1, ncx):
        pl.semaphore_signal(
            barrier, inc=1, device_id=(lax.rem(cx + k, ncx), cy), device_id_type=MESH
        )
    for k in range(1, ncy):
        pl.semaphore_signal(
            barrier, inc=1, device_id=(cx, lax.rem(cy + k, ncy)), device_id_type=MESH
        )
    in_copies[0].wait()
    halo_out[0] = latent[:, 0:LANES].astype(BF16)
    halo_out[1] = latent[:, LANES:].astype(BF16)
    pl.semaphore_wait(barrier, ncx + ncy - 2)
    for k in range(1, ncx):
        pl.semaphore_signal(
            ready, inc=1, device_id=(lax.rem(cx + k, ncx), cy), device_id_type=MESH
        )

    def start_halo(at, along):
        copies = []
        for side in range(2):
            step = 1 if side == 0 else -1
            if along == "x":
                to = (lax.rem(cx + step + ncx, ncx), cy)
            else:
                to = (cx, lax.rem(cy + step + ncy, ncy))
            copy = pltpu.make_async_remote_copy(
                src_ref=halo_out.at[at],
                dst_ref=halo_in.at[2 * at + side],
                send_sem=halo_send.at[2 * at + side],
                recv_sem=halo_recv.at[2 * at + side],
                device_id=to,
                device_id_type=MESH,
            )
            copy.start()
            copies.append(copy)
        return copies

    def own_part(x, at):
        both = dot(tabs[2 * at], jnp.concatenate(split(x), axis=1))
        return both[:, :LANES] + both[:, LANES:] + dot(tabs[2 * at + 1], x.astype(BF16))

    def halo_part(copies, at, first):
        place, count = (cx, ncx) if first == 0 else (cy, ncy)
        copies[0].wait_recv()
        copies[1].wait_recv()
        left = halo_in[2 * at]
        right = halo_in[2 * at + 1]
        from_left = dot(tabs[2 * first + 2], left) + dot(tabs[2 * first + 3], left)
        from_right = dot(tabs[2 * first + 4], right) + dot(tabs[2 * first + 5], right)
        zero = jnp.zeros_like(from_left)
        return jnp.where(place > 0, from_left, zero) + jnp.where(
            place < count - 1, from_right, zero
        )

    def along_z(x):
        high, low = split(x)
        return dot(high, tabs[12]) + dot(high, tabs[13]) + dot(low, tabs[12])

    count = ncx * ncy
    me = cx * ncy + cy
    ring_x = 4 if ncy % 4 == 0 else ncy
    ring_y, ring_z = ncy // ring_x, ncx // 2
    at_z, at_core = cx // 2, lax.rem(cx, 2)
    at_y, at_x = cy // ring_x, lax.rem(cy, ring_x)

    def start_swap(out, into, at):
        for dz, dc, dy, dx in far_first(ring_z, ring_y, ring_x):
            to_cx = lax.rem(at_z + dz, ring_z) * 2 + lax.rem(at_core + dc, 2)
            to_cy = lax.rem(at_y + dy, ring_y) * ring_x + lax.rem(at_x + dx, ring_x)
            pltpu.make_async_remote_copy(
                src_ref=out.at[to_cx * ncy + to_cy],
                dst_ref=into.at[me],
                send_sem=swap_send.at[at],
                recv_sem=swap_recv.at[at],
                device_id=(to_cx, to_cy),
                device_id_type=MESH,
            ).start()
        into[me] = out[me]

    def all_but_one(ref, sem):
        part = ref.at[pl.ds(0, count - 1)]
        return pltpu.make_async_copy(part, part, sem)

    started = []

    def smooth(x, base, first_work, second_work):
        low, high = x[:, :LANES], x[:, LANES:]
        if base > 0:
            halo_out[base] = low.astype(BF16)
            halo_out[base + 1] = high.astype(BF16)
        low_copies = start_halo(base, "x")
        high_copies = start_halo(base + 1, "y")
        started.extend(low_copies + high_copies)
        first_work()
        low, high = own_part(low, 0), own_part(high, 3)
        low = low + halo_part(low_copies, base, 0)
        halo_out[base + 2] = low.astype(BF16)
        low_copies = start_halo(base + 2, "y")
        high = high + halo_part(high_copies, base + 1, 3)
        halo_out[base + 3] = high.astype(BF16)
        high_copies = start_halo(base + 3, "x")
        started.extend(low_copies + high_copies)
        second_work()
        low, high = own_part(low, 3), own_part(high, 0)
        high = high + halo_part(high_copies, base + 3, 0)
        low = low + halo_part(low_copies, base + 2, 3)
        return along_z(jnp.concatenate([low, high], axis=1))


    def columns_of(row):
        return jnp.broadcast_to(row.astype(F32), (LANES, row.shape[1])).T

    lane_of = lax.broadcasted_iota(jnp.int32, (1, LANES), 1).astype(F32)
    voxels = latent.shape[0]
    depth = latent.shape[1]
    group_rows = 8 * samples
    groups = observed.shape[0]

    def prepare(g, carry):
        rows = pl.ds(pl.multiple_of(g * group_rows, group_rows), group_rows)
        resp_t[g] = resp[rows, :].T
        first = g * 8
        strip = low_index[:, pl.ds(pl.multiple_of(first // LANES * LANES, LANES), LANES)]
        hots = []
        for t in range(8):
            lane = jnp.full((samples, LANES), lax.rem(first, LANES) + t, jnp.int32)
            at = jnp.take_along_axis(strip, lane, axis=1, mode="promise_in_bounds")
            hots.append(one_hot(at, lane_of))
        hot_near[rows, :] = jnp.concatenate(hots, axis=0)
        return carry

    steps = tiles // 8
    per_chunk = steps // len(resp_copies)

    def prepare_chunks(chunks):
        for i in chunks:
            resp_copies[i].wait()
            lax.fori_loop(i * per_chunk, (i + 1) * per_chunk, prepare, 0, unroll=4)

    def index_work():
        for copy in in_copies[1:]:
            copy.wait()
        owner = lax.broadcasted_iota(jnp.int32, (count, 1), 0)
        slot_lane = lax.broadcasted_iota(jnp.int32, (1, slots), 1)
        spread = dot(
            jnp.concatenate([send[...].astype(F32), jnp.zeros((8 - cap, count), F32)], axis=0).astype(BF16),
            one_hot(owner, slot_lane // cap),
        )
        own_lane = lax.broadcasted_iota(jnp.int32, (8, 1), 0) == lax.rem(slot_lane, cap)
        send_row = jnp.sum(jnp.where(own_lane, spread, 0.0), axis=0, keepdims=True)
        send_col = columns_of(send_row)
        for j in range(voxels // LANES):
            hot_out[:, j * LANES : (j + 1) * LANES] = one_hot(send_col, lane_of + j * LANES)
        row_of = lax.broadcasted_iota(jnp.int32, (voxels, 1), 0).astype(F32)
        hot_back[...] = one_hot(row_of, send_row)
        slot_row = lax.broadcasted_iota(jnp.int32, (slots, 1), 0).astype(F32)
        hot_slot[...] = one_hot(slot_row, slot[...].astype(F32))
        below = offsets[...].astype(F32)
        index[...] = jnp.concatenate([below, below + 1.0], axis=0).T.astype(jnp.int32)
        odup[...] = jnp.concatenate([below, below], axis=0).T
        share = fractions[...]
        weight[...] = jnp.concatenate([1.0 - share, share], axis=0).T
        low_index[...] = jnp.where(below >= LANES, below - LANES, below)
        group_of = lax.broadcasted_iota(jnp.int32, (groups, 1), 0).astype(F32)
        hot_group[...] = one_hot(group_of, group[...].astype(F32))
        hot_of_tile[...] = one_hot(columns_of(group[...]), lane_of)
        tab_copy.wait()
        prepare_chunks(CHUNKS_X)

    field = smooth(latent[...], 0, index_work, lambda: prepare_chunks(CHUNKS_Y))
    dens = jnp.exp(field)
    density[...] = dens

    packed = dot(hot_out[...], dens.astype(BF16)).astype(BF16)
    there_out[...] = packed.reshape(there_out.shape)
    pl.semaphore_wait(ready, ncx - 1)
    start_swap(there_out, there_in, 0)
    prepare_chunks(CHUNKS_SWAP)
    slot_col = columns_of(slot[...])
    hot_tile = jnp.concatenate(
        [one_hot(slot_col, lane_of + j * LANES) for j in range(-(-slots // LANES))], axis=1
    )[:, :slots]
    all_but_one(there_in, swap_recv.at[0]).wait()
    block_of[...] = dot(hot_tile, there_in[...].reshape(slots, depth))

    pair_of = lax.broadcasted_iota(jnp.int32, (8, LANES), 0) // 2
    odd_row = lax.rem(lax.broadcasted_iota(jnp.int32, (8, LANES), 0), 2)
    upper = lax.broadcasted_iota(jnp.int32, (8, LANES), 1) // samples
    keep = [(pair_of == j) & (odd_row == upper) for j in range(4)]
    masks = [jnp.where(k, 1.0, 0.0) for k in keep]
    high_lane = lax.broadcasted_iota(jnp.int32, (1, LANES), 1) >= samples
    masks = [m.astype(BF16) for m in masks]
    set_of = 8 * SET

    def forward(i, carry):
        first = pl.multiple_of(i * set_of, set_of)
        rows = pl.ds(first, set_of)
        at = index[rows, :]
        near = at & (LANES - 1)
        low = jnp.take_along_axis(
            block_of[rows, 0:LANES], near, axis=1, mode="promise_in_bounds"
        )
        far = jnp.take_along_axis(
            block_of[rows, LANES : 2 * LANES], near, axis=1, mode="promise_in_bounds"
        )
        terms = jnp.where(at < LANES, low, far) * weight[rows, :]
        sample = (terms + pltpu.roll(terms, samples, 1)).astype(BF16)
        lefts = []
        for j in range(SET):
            own = sample[8 * j : 8 * j + 8]
            lefts.append(jnp.concatenate([own * m for m in masks], axis=1))
        preds = []
        for j in range(SET):
            at_row = pl.multiple_of(first * samples + j * group_rows, group_rows)
            preds.append(dot(lefts[j], resp[pl.ds(at_row, group_rows), :]))
        tile_pred[rows, :] = jnp.concatenate(preds, axis=0)
        return carry

    lax.fori_loop(0, tiles // set_of, forward, 0)

    high, low = split(tile_pred[...])
    total = dot(hot_group[...], high) + dot(hot_group[...], low)
    predicted[...] = total
    resid = (total - observed[...]) / (sigma[...] * sigma[...])
    resid = jnp.concatenate([resid, jnp.zeros((LANES - groups, LANES), F32)], axis=0)
    tile_resid[...] = dot(hot_of_tile[...], resid.astype(BF16))

    masks2 = [jnp.concatenate([m, m], axis=0) for m in masks]

    def backward(i, carry):
        first = pl.multiple_of(i * set_of, set_of)
        rows = pl.ds(first, set_of)
        tr = tile_resid[rows, :].astype(BF16)
        backs = [dot(tr[8 * j : 8 * j + 8], resp_t[i * SET + j]) for j in range(SET)]
        own = jnp.concatenate(
            [
                sum(
                    jnp.where(keep[n], back[:, n * LANES : (n + 1) * LANES], 0.0)
                    for n in range(4)
                )
                for back in backs
            ],
            axis=0,
        )
        own = own + pltpu.roll(own, samples, 1)
        parts = own * weight[rows, :]
        turned = pltpu.roll(parts, samples, 1)
        v_low = jnp.where(high_lane, turned, parts)
        v_high = jnp.where(high_lane, parts, turned)
        is_far = odup[rows, :] >= LANES
        kinds = [
            jnp.where(is_far, 0.0, v_low),
            jnp.where(is_far, 0.0, v_high),
            jnp.where(is_far, v_low, 0.0),
            jnp.where(is_far, v_high, 0.0),
        ]
        lefts = []
        for j in range(SET):
            own_kinds = [kind[8 * j : 8 * j + 8] for kind in kinds]
            near = jnp.concatenate(own_kinds[0:2], axis=0).astype(BF16)
            far = jnp.concatenate(own_kinds[2:4], axis=0).astype(BF16)
            lefts.append(
                jnp.concatenate(
                    [
                        jnp.concatenate([near * m for m in masks2], axis=1),
                        jnp.concatenate([far * m for m in masks2], axis=1),
                    ],
                    axis=0,
                )
            )
        outs = []
        for j in range(SET):
            at_row = pl.multiple_of(first * samples + j * group_rows, group_rows)
            outs.append(dot(lefts[j], hot_near[pl.ds(at_row, group_rows), :]))
        lower_near = jnp.concatenate([out[0:8] for out in outs], axis=0)
        raised_near = jnp.concatenate([out[8:16] for out in outs], axis=0)
        lower_far = jnp.concatenate([out[16:24] for out in outs], axis=0)
        raised_far = jnp.concatenate([out[24:32] for out in outs], axis=0)
        raised = jnp.concatenate([raised_near, raised_far], axis=1)
        lower = jnp.concatenate([lower_near, lower_far], axis=1)
        tile_grad[rows, :] = lower + pltpu.roll(raised, 1, 1)
        return carry

    lax.fori_loop(0, tiles // set_of, backward, 0)

    high, low = split(tile_grad[...])
    slot_grad = dot(hot_slot[...], high) + dot(hot_slot[...], low)

    back_out[...] = slot_grad.astype(BF16).reshape(back_out.shape)
    start_swap(back_out, back_in, 1)
    all_but_one(back_in, swap_recv.at[1]).wait()
    dens_grad = dot(hot_back[...], back_in[...].reshape(slots, depth))

    field = density[...] * dens_grad
    field = smooth(field, 4, lambda: None, lambda: None)
    gradient[...] = latent[...] + field
    for copy in started:
        copy.wait_send()
    all_but_one(there_out, swap_send.at[0]).wait()
    all_but_one(back_out, swap_send.at[1]).wait()


def hand_out(field, stars, field_out, stars_out):
    field_out[...] = field[...]
    stars_out[...] = stars[...]


def on_device(
    latent, observed, sigma, response, offsets, fractions, tile_group, tile_slot, send_index
):
    ncx, ncy = lax.axis_size("cx"), lax.axis_size("cy")
    rows_x, rows_y, depth = latent.shape
    tiles, samples, star_tile = response.shape
    groups = observed.shape[0] // star_tile
    cap = send_index.shape[2]
    voxels = rows_x * rows_y
    slots = ncx * ncy * cap
    tables = smoothing_tables(rows_x, rows_y, depth)
    chunks = 16
    vmem = pl.BlockSpec(memory_space=pltpu.VMEM)
    anywhere = pl.BlockSpec(memory_space=pltpu.HBM)
    gradient, predicted = pl.pallas_call(
        functools.partial(kernel, ncx, ncy, cap),
        out_shape=(
            jax.ShapeDtypeStruct((voxels, depth), F32),
            jax.ShapeDtypeStruct((groups, star_tile), F32),
        ),
        in_specs=[anywhere] * 10,
        out_specs=(vmem, vmem),
        scratch_shapes=[
            pltpu.VMEM((voxels, depth), F32),
            pltpu.VMEM((groups, star_tile), F32),
            pltpu.VMEM((groups, star_tile), F32),
            pltpu.VMEM((samples, tiles), jnp.int32),
            pltpu.VMEM((samples, tiles), F32),
            pltpu.VMEM((1, tiles), jnp.int32),
            pltpu.VMEM((1, tiles), jnp.int32),
            pltpu.VMEM((cap, ncx * ncy), jnp.int32),
            pltpu.VMEM((tiles * samples, star_tile), BF16),
            pltpu.VMEM((tiles // 8, star_tile, 8 * samples), BF16),
            pltpu.VMEM((tiles * samples, LANES), BF16),
            pltpu.VMEM(tables.shape, BF16),
            pltpu.VMEM((8, voxels, depth // 2), BF16),
            pltpu.VMEM((16, voxels, depth // 2), BF16),
            pltpu.VMEM((ncx * ncy, cap, depth), BF16),
            pltpu.VMEM((ncx * ncy, cap, depth), BF16),
            pltpu.VMEM((ncx * ncy, cap, depth), BF16),
            pltpu.VMEM((ncx * ncy, cap, depth), BF16),
            pltpu.VMEM((tiles, 2 * samples), jnp.int32),
            pltpu.VMEM((tiles, 2 * samples), F32),
            pltpu.VMEM((tiles, 2 * samples), F32),
            pltpu.VMEM((samples, tiles), F32),
            pltpu.VMEM((tiles, depth), F32),
            pltpu.VMEM((tiles, star_tile), F32),
            pltpu.VMEM((tiles, star_tile), F32),
            pltpu.VMEM((tiles, depth), F32),
            pltpu.VMEM((slots, voxels), BF16),
            pltpu.VMEM((voxels, slots), BF16),
            pltpu.VMEM((slots, tiles), BF16),
            pltpu.VMEM((groups, tiles), BF16),
            pltpu.VMEM((tiles, LANES), BF16),
            pltpu.VMEM((voxels, depth), F32),
            pltpu.SemaphoreType.DMA((8,)),
            pltpu.SemaphoreType.DMA((chunks,)),
            pltpu.SemaphoreType.DMA,
            pltpu.SemaphoreType.DMA((16,)),
            pltpu.SemaphoreType.DMA((16,)),
            pltpu.SemaphoreType.DMA((2,)),
            pltpu.SemaphoreType.DMA((2,)),
            pltpu.SemaphoreType.REGULAR,
        ],
        compiler_params=pltpu.CompilerParams(
            collective_id=0, has_side_effects=True, vmem_limit_bytes=62 * 1024 * 1024
        ),
        name="dust_map",
    )(
        latent.reshape(voxels, depth),
        observed.reshape(groups, star_tile),
        sigma.reshape(groups, star_tile),
        response.reshape(tiles * samples, star_tile),
        offsets,
        fractions,
        tile_group.reshape(1, tiles),
        tile_slot.reshape(1, tiles),
        send_index.transpose(0, 2, 1).reshape(cap, ncx * ncy),
        jnp.asarray(tables),
    )
    gradient, predicted = pl.pallas_call(
        hand_out,
        out_shape=(
            jax.ShapeDtypeStruct((voxels, depth), F32),
            jax.ShapeDtypeStruct((groups, star_tile), F32),
        ),
        in_specs=[vmem] * 2,
        out_specs=(vmem, vmem),
        name="hand_out",
    )(gradient, predicted)
    return gradient.reshape(latent.shape), predicted.reshape(-1)


def solution(mesh):
    placed = (
        P("cx", "cy", None),
        P(("cx", "cy")),
        P(("cx", "cy")),
        P(("cx", "cy"), None, None),
        P(None, ("cx", "cy")),
        P(None, ("cx", "cy")),
        P(("cx", "cy")),
        P(("cx", "cy")),
        P(("cx", "cy"), None, None),
    )
    return jax.shard_map(
        on_device,
        mesh=mesh,
        in_specs=placed,
        out_specs=(P("cx", "cy", None), P(("cx", "cy"))),
        check_vma=False,
    )
```

```python
import functools
import itertools

import jax
import jax.numpy as jnp
import ml_dtypes
import numpy as np
from jax import lax
from jax.experimental import pallas as pl
from jax.experimental.pallas import tpu as pltpu
from jax.sharding import PartitionSpec as P

F32, BF16 = jnp.float32, jnp.bfloat16
MESH = pl.DeviceIdType.MESH
LANES = 128
SET = 64
CHUNKS_X, CHUNKS_Y, CHUNKS_SWAP = tuple(range(2)), tuple(range(2, 6)), tuple(range(6, 16))


def smoothing_tables(rows_x, rows_y, depth):
    shifts = np.arange(-16, 17).astype(np.float32)
    scaled = np.sqrt(np.float32(3.0)) * np.abs(shifts) / np.float32(8.0)
    raw = (np.float32(1.0) + scaled) * np.exp(-scaled)
    taps = np.float32(0.8) * raw / np.sqrt(np.sum(raw * raw))

    def band(length, start):
        shift = np.arange(length)[None, :] + start - np.arange(length)[:, None]
        inside = np.abs(shift) <= 16
        return np.where(inside, taps[np.clip(shift + 16, 0, 32)], 0).astype(np.float32)

    whole = [np.kron(band(rows_x, s), np.eye(rows_y)) for s in (0, -rows_x, rows_x)]
    whole += [np.kron(np.eye(rows_x), band(rows_y, s)) for s in (0, -rows_y, rows_y)]
    whole += [band(depth, 0)]
    parts = []
    for table in whole:
        table = table.astype(np.float32)
        high = table.astype(ml_dtypes.bfloat16)
        parts += [high, (table - high.astype(np.float32)).astype(ml_dtypes.bfloat16)]
    return np.stack(parts)


def dot(a, b):
    return lax.dot_general(a, b, (((1,), (0,)), ((), ())), preferred_element_type=F32)


def dot_t(a, b):
    return lax.dot_general(a, b, (((1,), (1,)), ((), ())), preferred_element_type=F32)


def split(x):
    high = x.astype(BF16)
    return high, (x - high.astype(F32)).astype(BF16)


def one_hot(a, b):
    return jnp.where(a == b, 1.0, 0.0).astype(BF16)


def far_first(ring_z, ring_y, ring_x):
    def links(step):
        dz, dc, dy, dx = step
        return (
            min(dz, ring_z - dz) + min(dy, ring_y - dy) + min(dx, ring_x - dx) + 0.5 * dc
        )

    steps = itertools.product(range(ring_z), range(2), range(ring_y), range(ring_x))
    return sorted((step for step in steps if any(step)), key=links, reverse=True)


def kernel(
    ncx, ncy, cap,
    latent_hbm, observed_hbm, sigma_hbm, response, offsets_hbm, fractions_hbm, group_hbm,
    slot_hbm, send_hbm, tables,
    gradient, predicted,
    latent, observed, sigma, offsets, fractions, group, slot, send, resp, resp_t, hot_near, tabs,
    halo_out, halo_in, there_out, there_in, back_out, back_in,
    index, weight, odup, low_index, block_of, tile_pred, tile_resid, tile_grad,
    hot_out, hot_back, hot_slot, hot_group, hot_of_tile, density,
    in_sem, resp_sem, tab_sem, halo_send, halo_recv, swap_send, swap_recv, ready,
):
    cx, cy = lax.axis_index("cx"), lax.axis_index("cy")
    tiles = slot.shape[1]
    slots = ncx * ncy * cap
    samples = offsets.shape[0]
    chunk_rows = resp.shape[0] // resp_sem.shape[0]

    in_copies = [
        pltpu.make_async_copy(source, target, in_sem.at[i])
        for i, (source, target) in enumerate(
            [
                (latent_hbm, latent),
                (send_hbm, send),
                (slot_hbm, slot),
                (offsets_hbm, offsets),
                (fractions_hbm, fractions),
                (group_hbm, group),
                (observed_hbm, observed),
                (sigma_hbm, sigma),
            ]
        )
    ]
    in_copies[0].start()
    barrier = pltpu.get_barrier_semaphore()
    for k in range(1, ncx):
        pl.semaphore_signal(
            barrier, inc=1, device_id=(lax.rem(cx + k, ncx), cy), device_id_type=MESH
        )
    for k in range(1, ncy):
        pl.semaphore_signal(
            barrier, inc=1, device_id=(cx, lax.rem(cy + k, ncy)), device_id_type=MESH
        )
    for copy in in_copies[1:]:
        copy.start()
    tab_copy = pltpu.make_async_copy(tables, tabs, tab_sem)
    tab_copy.start()
    resp_copies = [
        pltpu.make_async_copy(
            response.at[pl.ds(i * chunk_rows, chunk_rows)],
            resp.at[pl.ds(i * chunk_rows, chunk_rows)],
            resp_sem.at[i],
        )
        for i in range(resp_sem.shape[0])
    ]
    for copy in resp_copies:
        copy.start()

    in_copies[0].wait()
    halo_out[0] = latent[:, 0:LANES].astype(BF16)
    halo_out[1] = latent[:, LANES:].astype(BF16)
    pl.semaphore_wait(barrier, ncx + ncy - 2)

    def start_halo(at, along):
        copies = []
        for side in range(2):
            step = 1 if side == 0 else -1
            if along == "x":
                to = (lax.rem(cx + step + ncx, ncx), cy)
            else:
                to = (cx, lax.rem(cy + step + ncy, ncy))
            copy = pltpu.make_async_remote_copy(
                src_ref=halo_out.at[at],
                dst_ref=halo_in.at[2 * at + side],
                send_sem=halo_send.at[2 * at + side],
                recv_sem=halo_recv.at[2 * at + side],
                device_id=to,
                device_id_type=MESH,
            )
            copy.start()
            copies.append(copy)
        return copies

    def own_part(x, at):
        both = dot(tabs[2 * at], jnp.concatenate(split(x), axis=1))
        return both[:, :LANES] + both[:, LANES:] + dot(tabs[2 * at + 1], x.astype(BF16))

    def halo_part(copies, at, first):
        place, count = (cx, ncx) if first == 0 else (cy, ncy)
        copies[0].wait_recv()
        copies[1].wait_recv()
        left = halo_in[2 * at]
        right = halo_in[2 * at + 1]
        from_left = dot(tabs[2 * first + 2], left) + dot(tabs[2 * first + 3], left)
        from_right = dot(tabs[2 * first + 4], right) + dot(tabs[2 * first + 5], right)
        zero = jnp.zeros_like(from_left)
        return jnp.where(place > 0, from_left, zero) + jnp.where(
            place < count - 1, from_right, zero
        )

    def along_z(x):
        high, low = split(x)
        return dot(high, tabs[12]) + dot(high, tabs[13]) + dot(low, tabs[12])

    count = ncx * ncy
    me = cx * ncy + cy
    ring_x = 4 if ncy % 4 == 0 else ncy
    ring_y, ring_z = ncy // ring_x, ncx // 2
    at_z, at_core = cx // 2, lax.rem(cx, 2)
    at_y, at_x = cy // ring_x, lax.rem(cy, ring_x)

    def start_swap(out, into, at):
        for dz, dc, dy, dx in far_first(ring_z, ring_y, ring_x):
            to_cx = lax.rem(at_z + dz, ring_z) * 2 + lax.rem(at_core + dc, 2)
            to_cy = lax.rem(at_y + dy, ring_y) * ring_x + lax.rem(at_x + dx, ring_x)
            pltpu.make_async_remote_copy(
                src_ref=out.at[to_cx * ncy + to_cy],
                dst_ref=into.at[me],
                send_sem=swap_send.at[at],
                recv_sem=swap_recv.at[at],
                device_id=(to_cx, to_cy),
                device_id_type=MESH,
            ).start()
        into[me] = out[me]

    def all_but_one(ref, sem):
        part = ref.at[pl.ds(0, count - 1)]
        return pltpu.make_async_copy(part, part, sem)

    started = []

    def smooth(x, base, first_work, second_work):
        low, high = x[:, :LANES], x[:, LANES:]
        if base > 0:
            halo_out[base] = low.astype(BF16)
            halo_out[base + 1] = high.astype(BF16)
        high_copies = start_halo(base + 1, "y")
        low_copies = start_halo(base, "x")
        started.extend(low_copies + high_copies)
        first_work()
        low, high = own_part(low, 0), own_part(high, 3)
        low = low + halo_part(low_copies, base, 0)
        halo_out[base + 2] = low.astype(BF16)
        low_copies = start_halo(base + 2, "y")
        high = high + halo_part(high_copies, base + 1, 3)
        halo_out[base + 3] = high.astype(BF16)
        high_copies = start_halo(base + 3, "x")
        started.extend(low_copies + high_copies)
        second_work()
        low, high = own_part(low, 3), own_part(high, 0)
        high = high + halo_part(high_copies, base + 3, 0)
        low = low + halo_part(low_copies, base + 2, 3)
        return along_z(jnp.concatenate([low, high], axis=1))


    def columns_of(row):
        return jnp.broadcast_to(row.astype(F32), (LANES, row.shape[1])).T

    lane_of = lax.broadcasted_iota(jnp.int32, (1, LANES), 1).astype(F32)
    voxels = latent.shape[0]
    depth = latent.shape[1]
    group_rows = 8 * samples
    groups = observed.shape[0]

    def prepare(g, carry):
        rows = pl.ds(pl.multiple_of(g * group_rows, group_rows), group_rows)
        resp_t[g] = resp[rows, :].T
        first = g * 8
        strip = low_index[:, pl.ds(pl.multiple_of(first // LANES * LANES, LANES), LANES)]
        hots = []
        for t in range(8):
            lane = jnp.full((samples, LANES), lax.rem(first, LANES) + t, jnp.int32)
            at = jnp.take_along_axis(strip, lane, axis=1, mode="promise_in_bounds")
            hots.append(one_hot(at, lane_of))
        hot_near[rows, :] = jnp.concatenate(hots, axis=0)
        return carry

    steps = tiles // 8
    per_chunk = steps // len(resp_copies)

    def prepare_chunks(chunks):
        for i in chunks:
            resp_copies[i].wait()
            lax.fori_loop(i * per_chunk, (i + 1) * per_chunk, prepare, 0, unroll=4)

    def index_work():
        for k in range(1, ncx):
            pl.semaphore_signal(
                ready, inc=1, device_id=(lax.rem(cx + k, ncx), cy), device_id_type=MESH
            )
        for copy in in_copies[1:]:
            copy.wait()
        owner = lax.broadcasted_iota(jnp.int32, (count, 1), 0)
        slot_lane = lax.broadcasted_iota(jnp.int32, (1, slots), 1)
        spread = dot(
            jnp.concatenate([send[...].astype(F32), jnp.zeros((8 - cap, count), F32)], axis=0).astype(BF16),
            one_hot(owner, slot_lane // cap),
        )
        own_lane = lax.broadcasted_iota(jnp.int32, (8, 1), 0) == lax.rem(slot_lane, cap)
        send_row = jnp.sum(jnp.where(own_lane, spread, 0.0), axis=0, keepdims=True)
        send_col = columns_of(send_row)
        for j in range(voxels // LANES):
            hot_out[:, j * LANES : (j + 1) * LANES] = one_hot(send_col, lane_of + j * LANES)
        row_of = lax.broadcasted_iota(jnp.int32, (voxels, 1), 0).astype(F32)
        hot_back[...] = one_hot(row_of, send_row)
        slot_row = lax.broadcasted_iota(jnp.int32, (slots, 1), 0).astype(F32)
        hot_slot[...] = one_hot(slot_row, slot[...].astype(F32))
        below = offsets[...].astype(F32)
        index[...] = jnp.concatenate([below, below + 1.0], axis=0).T.astype(jnp.int32)
        odup[...] = jnp.concatenate([below, below], axis=0).T
        share = fractions[...]
        weight[...] = jnp.concatenate([1.0 - share, share], axis=0).T
        low_index[...] = jnp.where(below >= LANES, below - LANES, below)
        group_of = lax.broadcasted_iota(jnp.int32, (groups, 1), 0).astype(F32)
        hot_group[...] = one_hot(group_of, group[...].astype(F32))
        hot_of_tile[...] = one_hot(columns_of(group[...]), lane_of)
        tab_copy.wait()
        prepare_chunks(CHUNKS_X)

    field = smooth(latent[...], 0, index_work, lambda: prepare_chunks(CHUNKS_Y))
    dens = jnp.exp(field)
    density[...] = dens

    packed = dot(hot_out[...], dens.astype(BF16)).astype(BF16)
    there_out[...] = packed.reshape(there_out.shape)
    pl.semaphore_wait(ready, ncx - 1)
    start_swap(there_out, there_in, 0)
    prepare_chunks(CHUNKS_SWAP)
    slot_col = columns_of(slot[...])
    hot_tile = jnp.concatenate(
        [one_hot(slot_col, lane_of + j * LANES) for j in range(-(-slots // LANES))], axis=1
    )[:, :slots]
    all_but_one(there_in, swap_recv.at[0]).wait()
    block_of[...] = dot(hot_tile, there_in[...].reshape(slots, depth))

    pair_of = lax.broadcasted_iota(jnp.int32, (8, LANES), 0) // 2
    odd_row = lax.rem(lax.broadcasted_iota(jnp.int32, (8, LANES), 0), 2)
    upper = lax.broadcasted_iota(jnp.int32, (8, LANES), 1) // samples
    keep = [(pair_of == j) & (odd_row == upper) for j in range(4)]
    masks = [jnp.where(k, 1.0, 0.0) for k in keep]
    high_lane = lax.broadcasted_iota(jnp.int32, (1, LANES), 1) >= samples
    masks = [m.astype(BF16) for m in masks]
    set_of = 8 * SET

    def forward(i, carry):
        first = pl.multiple_of(i * set_of, set_of)
        rows = pl.ds(first, set_of)
        at = index[rows, :]
        near = at & (LANES - 1)
        low = jnp.take_along_axis(
            block_of[rows, 0:LANES], near, axis=1, mode="promise_in_bounds"
        )
        far = jnp.take_along_axis(
            block_of[rows, LANES : 2 * LANES], near, axis=1, mode="promise_in_bounds"
        )
        terms = jnp.where(at < LANES, low, far) * weight[rows, :]
        sample = (terms + pltpu.roll(terms, samples, 1)).astype(BF16)
        lefts = []
        for j in range(SET):
            own = sample[8 * j : 8 * j + 8]
            lefts.append(jnp.concatenate([own * m for m in masks], axis=1))
        preds = []
        for j in range(SET):
            at_row = pl.multiple_of(first * samples + j * group_rows, group_rows)
            preds.append(dot(lefts[j], resp[pl.ds(at_row, group_rows), :]))
        tile_pred[rows, :] = jnp.concatenate(preds, axis=0)
        return carry

    lax.fori_loop(0, tiles // set_of, forward, 0)

    high, low = split(tile_pred[...])
    total = dot(hot_group[...], high) + dot(hot_group[...], low)
    predicted[...] = total
    resid = (total - observed[...]) / (sigma[...] * sigma[...])
    resid = jnp.concatenate([resid, jnp.zeros((LANES - groups, LANES), F32)], axis=0)
    tile_resid[...] = dot(hot_of_tile[...], resid.astype(BF16))

    masks2 = [jnp.concatenate([m, m], axis=0) for m in masks]

    def backward(i, carry):
        first = pl.multiple_of(i * set_of, set_of)
        rows = pl.ds(first, set_of)
        tr = tile_resid[rows, :].astype(BF16)
        backs = [dot(tr[8 * j : 8 * j + 8], resp_t[i * SET + j]) for j in range(SET)]
        own = jnp.concatenate(
            [
                sum(
                    jnp.where(keep[n], back[:, n * LANES : (n + 1) * LANES], 0.0)
                    for n in range(4)
                )
                for back in backs
            ],
            axis=0,
        )
        own = own + pltpu.roll(own, samples, 1)
        parts = own * weight[rows, :]
        turned = pltpu.roll(parts, samples, 1)
        v_low = jnp.where(high_lane, turned, parts)
        v_high = jnp.where(high_lane, parts, turned)
        is_far = odup[rows, :] >= LANES
        kinds = [
            jnp.where(is_far, 0.0, v_low),
            jnp.where(is_far, 0.0, v_high),
            jnp.where(is_far, v_low, 0.0),
            jnp.where(is_far, v_high, 0.0),
        ]
        lefts = []
        for j in range(SET):
            own_kinds = [kind[8 * j : 8 * j + 8] for kind in kinds]
            near = jnp.concatenate(own_kinds[0:2], axis=0).astype(BF16)
            far = jnp.concatenate(own_kinds[2:4], axis=0).astype(BF16)
            lefts.append(
                jnp.concatenate(
                    [
                        jnp.concatenate([near * m for m in masks2], axis=1),
                        jnp.concatenate([far * m for m in masks2], axis=1),
                    ],
                    axis=0,
                )
            )
        outs = []
        for j in range(SET):
            at_row = pl.multiple_of(first * samples + j * group_rows, group_rows)
            outs.append(dot(lefts[j], hot_near[pl.ds(at_row, group_rows), :]))
        lower_near = jnp.concatenate([out[0:8] for out in outs], axis=0)
        raised_near = jnp.concatenate([out[8:16] for out in outs], axis=0)
        lower_far = jnp.concatenate([out[16:24] for out in outs], axis=0)
        raised_far = jnp.concatenate([out[24:32] for out in outs], axis=0)
        raised = jnp.concatenate([raised_near, raised_far], axis=1)
        lower = jnp.concatenate([lower_near, lower_far], axis=1)
        tile_grad[rows, :] = lower + pltpu.roll(raised, 1, 1)
        return carry

    lax.fori_loop(0, tiles // set_of, backward, 0)

    high, low = split(tile_grad[...])
    slot_grad = dot(hot_slot[...], high) + dot(hot_slot[...], low)

    back_out[...] = slot_grad.astype(BF16).reshape(back_out.shape)
    start_swap(back_out, back_in, 1)
    all_but_one(back_in, swap_recv.at[1]).wait()
    dens_grad = dot(hot_back[...], back_in[...].reshape(slots, depth))

    field = density[...] * dens_grad
    field = smooth(field, 4, lambda: None, lambda: None)
    gradient[...] = latent[...] + field
    for copy in started:
        copy.wait_send()
    all_but_one(there_out, swap_send.at[0]).wait()
    all_but_one(back_out, swap_send.at[1]).wait()


def hand_out(field, stars, field_out, stars_out):
    field_out[...] = field[...]
    stars_out[...] = stars[...]


def on_device(
    latent, observed, sigma, response, offsets, fractions, tile_group, tile_slot, send_index
):
    ncx, ncy = lax.axis_size("cx"), lax.axis_size("cy")
    rows_x, rows_y, depth = latent.shape
    tiles, samples, star_tile = response.shape
    groups = observed.shape[0] // star_tile
    cap = send_index.shape[2]
    voxels = rows_x * rows_y
    slots = ncx * ncy * cap
    tables = smoothing_tables(rows_x, rows_y, depth)
    chunks = 16
    vmem = pl.BlockSpec(memory_space=pltpu.VMEM)
    anywhere = pl.BlockSpec(memory_space=pltpu.HBM)
    gradient, predicted = pl.pallas_call(
        functools.partial(kernel, ncx, ncy, cap),
        out_shape=(
            jax.ShapeDtypeStruct((voxels, depth), F32),
            jax.ShapeDtypeStruct((groups, star_tile), F32),
        ),
        in_specs=[anywhere] * 10,
        out_specs=(vmem, vmem),
        scratch_shapes=[
            pltpu.VMEM((voxels, depth), F32),
            pltpu.VMEM((groups, star_tile), F32),
            pltpu.VMEM((groups, star_tile), F32),
            pltpu.VMEM((samples, tiles), jnp.int32),
            pltpu.VMEM((samples, tiles), F32),
            pltpu.VMEM((1, tiles), jnp.int32),
            pltpu.VMEM((1, tiles), jnp.int32),
            pltpu.VMEM((cap, ncx * ncy), jnp.int32),
            pltpu.VMEM((tiles * samples, star_tile), BF16),
            pltpu.VMEM((tiles // 8, star_tile, 8 * samples), BF16),
            pltpu.VMEM((tiles * samples, LANES), BF16),
            pltpu.VMEM(tables.shape, BF16),
            pltpu.VMEM((8, voxels, depth // 2), BF16),
            pltpu.VMEM((16, voxels, depth // 2), BF16),
            pltpu.VMEM((ncx * ncy, cap, depth), BF16),
            pltpu.VMEM((ncx * ncy, cap, depth), BF16),
            pltpu.VMEM((ncx * ncy, cap, depth), BF16),
            pltpu.VMEM((ncx * ncy, cap, depth), BF16),
            pltpu.VMEM((tiles, 2 * samples), jnp.int32),
            pltpu.VMEM((tiles, 2 * samples), F32),
            pltpu.VMEM((tiles, 2 * samples), F32),
            pltpu.VMEM((samples, tiles), F32),
            pltpu.VMEM((tiles, depth), F32),
            pltpu.VMEM((tiles, star_tile), F32),
            pltpu.VMEM((tiles, star_tile), F32),
            pltpu.VMEM((tiles, depth), F32),
            pltpu.VMEM((slots, voxels), BF16),
            pltpu.VMEM((voxels, slots), BF16),
            pltpu.VMEM((slots, tiles), BF16),
            pltpu.VMEM((groups, tiles), BF16),
            pltpu.VMEM((tiles, LANES), BF16),
            pltpu.VMEM((voxels, depth), F32),
            pltpu.SemaphoreType.DMA((8,)),
            pltpu.SemaphoreType.DMA((chunks,)),
            pltpu.SemaphoreType.DMA,
            pltpu.SemaphoreType.DMA((16,)),
            pltpu.SemaphoreType.DMA((16,)),
            pltpu.SemaphoreType.DMA((2,)),
            pltpu.SemaphoreType.DMA((2,)),
            pltpu.SemaphoreType.REGULAR,
        ],
        compiler_params=pltpu.CompilerParams(
            collective_id=0, has_side_effects=True, vmem_limit_bytes=62 * 1024 * 1024
        ),
        name="dust_map",
    )(
        latent.reshape(voxels, depth),
        observed.reshape(groups, star_tile),
        sigma.reshape(groups, star_tile),
        response.reshape(tiles * samples, star_tile),
        offsets,
        fractions,
        tile_group.reshape(1, tiles),
        tile_slot.reshape(1, tiles),
        send_index.transpose(0, 2, 1).reshape(cap, ncx * ncy),
        jnp.asarray(tables),
    )
    gradient, predicted = pl.pallas_call(
        hand_out,
        out_shape=(
            jax.ShapeDtypeStruct((voxels, depth), F32),
            jax.ShapeDtypeStruct((groups, star_tile), F32),
        ),
        in_specs=[vmem] * 2,
        out_specs=(vmem, vmem),
        name="hand_out",
    )(gradient, predicted)
    return gradient.reshape(latent.shape), predicted.reshape(-1)


def solution(mesh):
    placed = (
        P("cx", "cy", None),
        P(("cx", "cy")),
        P(("cx", "cy")),
        P(("cx", "cy"), None, None),
        P(None, ("cx", "cy")),
        P(None, ("cx", "cy")),
        P(("cx", "cy")),
        P(("cx", "cy")),
        P(("cx", "cy"), None, None),
    )
    return jax.shard_map(
        on_device,
        mesh=mesh,
        in_specs=placed,
        out_specs=(P("cx", "cy", None), P(("cx", "cy"))),
        check_vma=False,
    )
```
